512 devices in a mesh: tm: 16 (over x, z_lo), space: 32 (over z_hi, y, core).
Axes of the slice: x: 4, y: 8, z: 8 (z_hi: 2, z_lo: 4; z = z_hi * 4 + z_lo), core: 2. Of those that a mesh axis runs over, the one named last changes fastest.
Arguments:
- volumes: bfloat16 [16, 1024, 4096], P('tm', 'space'), may hold values from -4 to 4
- shifts: int32 [2, 3, 16, 32], P(None, None, 'tm', 'space'), may hold values from -16 to 16
Outputs:
- correlations: float32 [2, 16, 32, 512], P(None, 'tm', 'space')
- registered: bfloat16 [16, 1024, 4096], P('tm', 'space')
- template: float32 [1024, 4096], P('space', 'tm')
The draws below stay inside these ranges and needn't reach their ends.
All inputs are finite; a program needn't handle non-finite values.
Results may differ from the reference program's by a relative error of at most 0.02.
Values may be sent and summed in bfloat16 or wider, within the bound.
A program may use at most 64 MiB of HBM per device.

```python
import math
import jax
import jax.numpy as jnp
from jax import lax

PL = 64
TX = 32
LAGS = 8
ITERS = 2
HALO = 16
V = 16
NPATCH = 32
NX = 1024


def draw_volumes(key, part):
    key = jax.random.fold_in(key, 7)
    key_rough = jax.random.fold_in(key, 1)
    full_shape = (V, NX, PL * PL)
    values = jnp.clip(jax.random.normal(key_rough, full_shape, jnp.float32), -4.0, 4.0)
    return values.astype(jnp.bfloat16)


def place_ends(values, key, least, high):
    spot = [jax.random.randint(jax.random.fold_in(key, axis), (), 0, length) for axis, length in enumerate(values.shape)]
    main_axis = values.shape.index(max(values.shape))
    next_to = spot[:main_axis] + [(spot[main_axis] + 1) % values.shape[main_axis]] + spot[main_axis + 1:]
    return values.at[tuple(spot)].set(least).at[tuple(next_to)].set(high)


def setup_inputs(seed: int = 0) -> dict:
    key_of = jax.random.split(jax.random.key(seed), 3)
    return {
        "volumes": draw_volumes(jax.random.fold_in(key_of[2], 71), 0),
        "shifts": place_ends(jax.random.randint(key_of[1], (ITERS, 3, V, NPATCH), -16, 17), jax.random.fold_in(key_of[1], 1), -16, 16).astype(jnp.int32),
    }


def dft_tables(length, lag_count):
    frequency = jnp.arange(length, dtype=jnp.int32)
    phases = (frequency[:, None] * frequency[None, :]) % length
    angles = phases.astype(jnp.float32) * (2.0 * math.pi / length)
    cosine = jnp.cos(angles)
    sine_tab = jnp.sin(angles)
    t_first = jnp.concatenate([cosine, -sine_tab], axis=0).astype(jnp.bfloat16)
    t_next = jnp.concatenate([jnp.concatenate([cosine, sine_tab], axis=1), jnp.concatenate([-sine_tab, cosine], axis=1)], axis=0).astype(jnp.bfloat16)
    lag_steps = jnp.arange(lag_count, dtype=jnp.int32) - lag_count // 2
    lag_phase = (lag_steps[:, None] * frequency[None, :]) % length
    lag_angles = lag_phase.astype(jnp.float32) * (2.0 * math.pi / length)
    lag_cos = jnp.cos(lag_angles)
    lag_sin = jnp.sin(lag_angles)
    inv_pair = jnp.concatenate([jnp.concatenate([lag_cos, -lag_sin], axis=1), jnp.concatenate([lag_sin, lag_cos], axis=1)], axis=0).astype(jnp.bfloat16)
    inv_real = jnp.concatenate([lag_cos, -lag_sin], axis=1).astype(jnp.bfloat16)
    return t_first, t_next, inv_pair, inv_real


def rotate_axes(array, stacked, leading, middle, trailing):
    return array.reshape(stacked, leading, middle, trailing).transpose(0, 2, 3, 1).reshape(stacked * middle, trailing * leading)


def first_section(t_first, patch_rows):
    return jnp.dot(t_first, patch_rows, preferred_element_type=jnp.float32).astype(jnp.bfloat16)


def later_sections(t_next, first_pass):
    length = first_pass.shape[0] // 2
    second = rotate_axes(first_pass, 2, length, length, length)
    third = rotate_axes(jnp.dot(t_next, second, preferred_element_type=jnp.float32).astype(jnp.bfloat16), 2, length, length, length)
    return rotate_axes(jnp.dot(t_next, third, preferred_element_type=jnp.float32).astype(jnp.bfloat16), 2, length, length, length)


def cross_spectrum(raw_spec, template_spec):
    length = raw_spec.shape[0] // 2
    raw_re = raw_spec[:length].astype(jnp.float32)
    raw_im = raw_spec[length:].astype(jnp.float32)
    tem_re = template_spec[:length].astype(jnp.float32)
    tem_im = template_spec[length:].astype(jnp.float32)
    return jnp.concatenate([raw_re * tem_re + raw_im * tem_im, raw_im * tem_re - raw_re * tem_im], axis=0).astype(jnp.bfloat16)


def lag_values(inv_pair, inv_real, crossed, lag_count):
    length = crossed.shape[0] // 2
    along_x = rotate_axes(jnp.dot(inv_pair, crossed, preferred_element_type=jnp.float32).astype(jnp.bfloat16), 2, lag_count, length, length)
    along_y = rotate_axes(jnp.dot(inv_pair, along_x, preferred_element_type=jnp.float32).astype(jnp.bfloat16), 2, lag_count, length, lag_count)
    along_z = jnp.dot(inv_real, along_y, preferred_element_type=jnp.float32)
    ordered = rotate_axes(along_z, 1, lag_count, lag_count, lag_count)
    return ordered.reshape(-1) * (1.0 / float(length) ** 6)


def warp_matrix(shift_one, n_out, n_in, offset):
    whole_cells = shift_one // 4
    fraction = (shift_one - 4 * whole_cells).astype(jnp.float32) * 0.25
    rows_idx = lax.broadcasted_iota(jnp.int32, (n_out, n_in), 0)
    cols_idx = lax.broadcasted_iota(jnp.int32, (n_out, n_in), 1)
    target = rows_idx + (offset - whole_cells)
    upper_weight = jnp.where(cols_idx == target, 1.0 - fraction, 0.0)
    lower_weight = jnp.where(cols_idx == target - 1, fraction, 0.0)
    return (upper_weight + lower_weight).astype(jnp.bfloat16)


def warp_patch(patch_rows, shift_vec, tile, length):
    across = warp_matrix(shift_vec[0], tile, length, (length - tile) // 2)
    shifted = jnp.dot(across, patch_rows, preferred_element_type=jnp.float32).astype(jnp.bfloat16).reshape(tile, length, length)
    second_mat = warp_matrix(shift_vec[1], length, length, 0)
    shifted = jnp.einsum("iy,xyz->xiz", second_mat.astype(jnp.float32), shifted.astype(jnp.float32)).astype(jnp.bfloat16)
    third_mat = warp_matrix(shift_vec[2], length, length, 0)
    shifted = jnp.einsum("iz,xyz->xyi", third_mat.astype(jnp.float32), shifted.astype(jnp.float32)).astype(jnp.bfloat16)
    return shifted.reshape(tile, length * length)


def reference(volumes, shifts):
    t_first, t_next, inv_pair, inv_real = dft_tables(PL, LAGS)
    padded = jnp.pad(volumes, ((0, 0), (HALO, HALO), (0, 0)))

    def warp_all(step_shifts):
        def one_volume(vol_index):
            def one_patch(patch_index):
                patch_rows = lax.dynamic_slice_in_dim(padded[vol_index], (patch_index * TX).astype(jnp.int32), PL, 0)
                return warp_patch(patch_rows, step_shifts[:, vol_index, patch_index], TX, PL)
            return lax.map(one_patch, jnp.arange(NPATCH, dtype=jnp.int32)).reshape(NX, PL * PL)
        return lax.map(one_volume, jnp.arange(V, dtype=jnp.int32))

    currents = [volumes]
    for iteration in range(ITERS):
        currents.append(warp_all(shifts[iteration]))
    templates = [jnp.sum(currents[iteration].astype(jnp.float32), axis=0) / V for iteration in range(ITERS)]
    padded_templates = jnp.pad(jnp.stack(templates).astype(jnp.bfloat16), ((0, 0), (HALO, HALO), (0, 0)))

    def per_patch(patch_index):
        row_start = (patch_index * TX).astype(jnp.int32)
        template_specs = [later_sections(t_next, first_section(t_first, lax.dynamic_slice_in_dim(padded_templates[iteration], row_start, PL, 0))) for iteration in range(ITERS)]

        def per_volume(vol_index):
            raw_spec = later_sections(t_next, first_section(t_first, lax.dynamic_slice_in_dim(padded[vol_index], row_start, PL, 0)))
            return jnp.stack([lag_values(inv_pair, inv_real, cross_spectrum(raw_spec, template_specs[iteration]), LAGS) for iteration in range(ITERS)])
        return lax.map(per_volume, jnp.arange(V, dtype=jnp.int32))

    correlations = lax.map(per_patch, jnp.arange(NPATCH, dtype=jnp.int32)).transpose(2, 1, 0, 3)
    return correlations, currents[ITERS], templates[ITERS - 1]
```

```python
import functools

import jax
import jax.numpy as jnp
from jax import lax
from jax.experimental import pallas as pl
from jax.experimental.pallas import tpu as pltpu
from jax.sharding import PartitionSpec as P

MESH = pl.DeviceIdType.MESH
F32, BF16, I32 = jnp.float32, jnp.bfloat16, jnp.int32

PL = 64
TX = 32
HALO = 16
NT = 16
COLS = 256
SIDES = tuple((dt, ds) for ds in (-1, 1, 0) for dt in (-1, 0, 1) if (dt, ds) != (0, 0))


def band(shift, delta):
    whole = jnp.right_shift(shift, 2)
    fraction = (shift - 4 * whole).astype(F32) * 0.25
    return jnp.where(
        delta == whole, 1.0 - fraction, jnp.where(delta == whole + 1, fraction, 0.0)
    )


def kernel(
    ns, vol_ref, shift_ref, corr_ref, reg_ref, tmpl_ref,
    patch, raw, across, planes, xw, cur, got, win, turned, rolled, lagged, part, gath,
    local_sem, halo_send, halo_recv, raw_send, raw_recv, rim_send, rim_recv,
    cur_send, cur_recv, win_send, win_recv, part_send, part_recv,
):
    t = lax.axis_index("tm")
    s = lax.axis_index("space")
    has_lo, has_hi = s > 0, s < ns - 1
    there = {-1: has_lo, 1: has_hi}
    from_side = {-1: has_hi, 1: has_lo}

    def across_tm(k):
        return lax.rem(t + k + NT, NT)

    def each_peer(body):
        def step(k, carry):
            body(k)
            return carry

        lax.fori_loop(1, NT, step, 0)

    def remote(src, dst, send, recv, peer):
        return pltpu.make_async_remote_copy(
            src_ref=src, dst_ref=dst, send_sem=send, recv_sem=recv,
            device_id=peer, device_id_type=MESH,
        )

    own = pltpu.make_async_copy(vol_ref.at[0], patch.at[pl.ds(HALO, TX)], local_sem)
    own.start()

    barrier = pltpu.get_barrier_semaphore()
    each_peer(
        lambda k: pl.semaphore_signal(
            barrier, inc=1, device_id=(across_tm(k), s), device_id_type=MESH
        )
    )
    for ds in (-1, 1):

        @pl.when(there[ds])
        def _():
            for dt in (-1, 0, 1):
                pl.semaphore_signal(
                    barrier, inc=1, device_id=(across_tm(dt), s + ds), device_id_type=MESH
                )

    row = lax.broadcasted_iota(I32, (TX, PL), 0)
    col = lax.broadcasted_iota(I32, (TX, PL), 1)
    a = lax.broadcasted_iota(I32, (COLS, COLS), 0)
    b = lax.broadcasted_iota(I32, (COLS, COLS), 1)
    for i in range(2):
        across[i] = band(shift_ref[i, 0, 0, 0], row + HALO - col).astype(BF16)
        third = band(shift_ref[i, 2, 0, 0], (b & 63) - (a & 63))
        for d in range(4):
            second = band(shift_ref[i, 1, 0, 0], (b >> 6) - (a >> 6) - 4 * (d - 2))
            planes[i, d] = (second * third).astype(BF16)
    xw[0:64] = jnp.zeros((64, COLS), BF16)
    xw[18 * TX : 19 * TX] = jnp.zeros((TX, COLS), BF16)
    for ds, at in ((-1, 0), (1, 48)):

        @pl.when(jnp.logical_not(there[ds]))
        def _():
            patch[at : at + HALO] = jnp.zeros((HALO, PL * PL), BF16)
            raw[:, at : at + HALO] = jnp.zeros((NT, HALO, COLS), BF16)
            win[:, :, at : at + HALO] = jnp.zeros((2, 3, HALO, COLS), BF16)

    own.wait()
    pl.semaphore_wait(barrier, NT - 1 + 3 * (has_lo.astype(I32) + has_hi.astype(I32)))

    def halo(ds):
        src, dst = (HALO, 48) if ds < 0 else (TX, 0)
        k = 0 if ds < 0 else 1
        return remote(
            patch.at[pl.ds(src, HALO)], patch.at[pl.ds(dst, HALO)],
            halo_send.at[k], halo_recv.at[k], (t, s + ds),
        )

    def raw_copy(k):
        to = across_tm(k)
        return remote(
            patch.at[pl.ds(HALO, TX), pl.ds(pl.multiple_of(to * COLS, COLS), COLS)],
            raw.at[t, pl.ds(HALO, TX)],
            raw_send.at[k], raw_recv.at[k], (to, s),
        )

    for ds in (-1, 1):
        pl.when(there[ds])(halo(ds).start)
    each_peer(lambda k: raw_copy(k).start())
    raw[t, HALO : HALO + TX] = patch[
        HALO : HALO + TX, pl.ds(pl.multiple_of(t * COLS, COLS), COLS)
    ]
    for ds in (-1, 1):
        pl.when(from_side[ds])(halo(ds).wait_recv)

    def warp(i):
        for c in range(NT):
            xw[(c + 2) * TX : (c + 3) * TX] = jnp.dot(
                across[i], patch[:, c * COLS : (c + 1) * COLS], preferred_element_type=F32
            ).astype(BF16)
        total = jnp.dot(xw[0 : NT * TX], planes[i, 0], preferred_element_type=F32)
        for d in range(1, 4):
            total += jnp.dot(
                xw[d * TX : (d + NT) * TX], planes[i, d], preferred_element_type=F32
            )
        return total.astype(BF16)

    cur[...] = warp(0).reshape(NT, TX, COLS)

    def cur_copy(k):
        to = across_tm(k)
        return remote(cur.at[to], got.at[t], cur_send.at[k], cur_recv.at[k], (to, s))

    each_peer(lambda k: cur_copy(k).start())
    got[t] = cur[t]

    def win_copy(i, side, act):
        dt, ds = SIDES[side]
        src = {0: HALO, -1: HALO, 1: TX}[ds]
        dst = {0: HALO, -1: 48, 1: 0}[ds]
        rows = TX if ds == 0 else HALO
        copy = remote(
            win.at[i, 1, pl.ds(src, rows)], win.at[i, 1 - dt, pl.ds(dst, rows)],
            win_send.at[i, side], win_recv.at[i, side], (across_tm(dt), s + ds),
        )
        present = (from_side if act == "wait_recv" else there).get(ds)
        if present is None:
            getattr(copy, act)()
        else:
            pl.when(present)(getattr(copy, act))

    def windows(i, mean):
        win[i, 1, HALO : HALO + TX] = mean.astype(BF16)
        for side in range(8):
            win_copy(i, side, "start")

    each_peer(lambda k: raw_copy(k).wait_recv())
    windows(0, jnp.sum(raw[:, HALO : HALO + TX].astype(F32), axis=0) * (1.0 / NT))

    def rim(ds):
        src, dst = (HALO, 48) if ds < 0 else (TX, 0)
        k = 0 if ds < 0 else 1
        return remote(
            raw.at[:, pl.ds(src, HALO)], raw.at[:, pl.ds(dst, HALO)],
            rim_send.at[k], rim_recv.at[k], (t, s + ds),
        )

    for ds in (-1, 1):
        pl.when(there[ds])(rim(ds).start)

    moved = warp(1)
    for c in range(NT):
        reg_ref[0, :, c * COLS : (c + 1) * COLS] = moved[c * TX : (c + 1) * TX]

    each_peer(lambda k: cur_copy(k).wait_recv())
    mean = jnp.sum(got[...].astype(F32), axis=0) * (1.0 / NT)
    tmpl_ref[...] = mean
    windows(1, mean)

    for ds in (-1, 1):
        pl.when(from_side[ds])(rim(ds).wait_recv)
    for j in range(8):
        rows16 = raw[:, 16 * (j // 2) : 16 * (j // 2) + 16].astype(F32)
        eight = rows16[:, 8 * (j % 2) : 8 * (j % 2) + 8].reshape(NT * 8, COLS)
        turned[j] = eight.T.astype(BF16)

    lane = lax.broadcasted_iota(I32, (2 * PL, 128), 1)
    place = lane & 63
    low_half = lane < 64
    step_of = lane & 7
    owner = lax.broadcasted_iota(I32, (NT, 128), 1) >> 3
    pick = (owner == lax.broadcasted_iota(I32, (NT, 128), 0)).astype(F32)

    def correlate(i):
        blocks = []
        for half in range(6):
            x = win[i, half // 2, :, 128 * (half % 2) : 128 * (half % 2) + 128].astype(F32)
            blocks.append(
                jnp.concatenate([pltpu.roll(x, 3, 0), pltpu.roll(x, PL - 5, 0)], axis=0)
            )

        for j3 in range(8):
            lag = j3 - 4
            turn = [pltpu.roll(x, lag % 128, 1) if lag else x for x in blocks]
            other = [pltpu.roll(x, (lag + 64) % 128, 1) for x in blocks]
            if lag > 0:
                inside = place >= lag
            else:
                inside = place < PL + lag
            even = [jnp.where(inside, p, q) for p, q in zip(turn, other)]
            swapped = [jnp.where(inside, q, p) for p, q in zip(turn, other)]
            odd = [
                jnp.where(low_half, swapped[h], swapped[h + 1]).astype(BF16) for h in range(5)
            ]
            even = [x.astype(BF16) for x in even]
            total = jnp.zeros((128, 128), F32)
            for j in range(8):
                rows = slice((j % 2) * PL + 16 * (j // 2), (j % 2) * PL + 16 * (j // 2) + 16)
                stack = []
                for j2 in range(8):
                    off = 8 - j2
                    which = odd if off % 2 else even
                    h = off // 2
                    stack.append(jnp.concatenate([which[h][rows], which[h + 1][rows]], axis=1))
                total += jnp.dot(
                    jnp.concatenate(stack, axis=0), turned[j], preferred_element_type=F32
                )
            for bit in (1, 2, 4):
                total = jnp.where((step_of & bit) != 0, pltpu.roll(total, 128 - bit, 0), total)
            lagged[j3 * 64 : (j3 + 1) * 64] = total.reshape(8, 16, 128)[:, 0:8].reshape(64, 128)
        ordered = jnp.concatenate(
            [
                lagged[pl.ds(j2 * 8 + 7 - j1, 8, stride=64), :]
                for j1 in range(8)
                for j2 in range(8)
            ],
            axis=0,
        )
        sums = lax.dot_general(
            pick, ordered, (((1,), (1,)), ((), ())),
            precision=lax.Precision.HIGHEST, preferred_element_type=F32,
        ) * (1.0 / float(PL) ** 3)
        for k in range(4):
            part[:, 4 * i + k, :] = sums[:, 128 * k : 128 * k + 128]

    for i in range(2):
        for side in range(8):
            win_copy(i, side, "wait_recv")
        correlate(i)

    def part_copy(k):
        to = across_tm(k)
        return remote(part.at[to], gath.at[t], part_send.at[k], part_recv.at[k], (to, s))

    each_peer(lambda k: part_copy(k).start())
    gath[t] = part[t]
    for ds in (-1, 1):
        pl.when(there[ds])(halo(ds).wait_send)
        pl.when(there[ds])(rim(ds).wait_send)
    each_peer(lambda k: raw_copy(k).wait_send())
    each_peer(lambda k: cur_copy(k).wait_send())
    for i in range(2):
        for side in range(8):
            win_copy(i, side, "wait_send")
    each_peer(lambda k: part_copy(k).wait_recv())
    final = jnp.sum(gath[...], axis=0)
    for i in range(2):
        for k in range(4):
            corr_ref[i, 0, :, 128 * k : 128 * k + 128] = final[4 * i + k : 4 * i + k + 1]
    each_peer(lambda k: part_copy(k).wait_send())


def solution(mesh):
    ns = mesh.shape["space"]

    def on_device(volumes, shifts):
        dma = pltpu.SemaphoreType.DMA
        vmem = pltpu.VMEM
        return pl.pallas_call(
            functools.partial(kernel, ns),
            out_shape=(
                jax.ShapeDtypeStruct((2, 1, 1, 512), F32),
                jax.ShapeDtypeStruct((1, TX, PL * PL), BF16),
                jax.ShapeDtypeStruct((TX, COLS), F32),
            ),
            in_specs=[
                pl.BlockSpec(memory_space=pl.ANY),
                pl.BlockSpec(memory_space=pltpu.SMEM),
            ],
            out_specs=(
                pl.BlockSpec(memory_space=pltpu.VMEM),
                pl.BlockSpec(memory_space=pltpu.VMEM),
                pl.BlockSpec(memory_space=pltpu.VMEM),
            ),
            scratch_shapes=[
                vmem((PL, PL * PL), BF16),
                vmem((NT, PL, COLS), BF16),
                vmem((2, TX, PL), BF16),
                vmem((2, 4, COLS, COLS), BF16),
                vmem(((NT + 3) * TX, COLS), BF16),
                vmem((NT, TX, COLS), BF16),
                vmem((NT, TX, COLS), BF16),
                vmem((2, 3, PL, COLS), BF16),
                vmem((8, COLS, 128), BF16),
                vmem((8, 128), F32),
                vmem((512, 128), F32),
                vmem((NT, 8, 128), F32),
                vmem((NT, 8, 128), F32),
                dma,
                dma((2,)), dma((2,)),
                dma((NT,)), dma((NT,)),
                dma((2,)), dma((2,)),
                dma((NT,)), dma((NT,)),
                dma((2, 8)), dma((2, 8)),
                dma((NT,)), dma((NT,)),
            ],
            compiler_params=pltpu.CompilerParams(
                collective_id=0, has_side_effects=True, vmem_limit_bytes=40 * 1024 * 1024
            ),
        )(volumes, shifts)

    return jax.shard_map(
        on_device,
        mesh=mesh,
        in_specs=(P("tm", "space", None), P(None, None, "tm", "space")),
        out_specs=(P(None, "tm", "space", None), P("tm", "space", None), P("space", "tm")),
        check_vma=False,
    )
```

```python
import functools

import jax
import jax.numpy as jnp
from jax import lax
from jax.experimental import pallas as pl
from jax.experimental.pallas import tpu as pltpu
from jax.sharding import PartitionSpec as P

MESH = pl.DeviceIdType.MESH
F32, BF16, I32 = jnp.float32, jnp.bfloat16, jnp.int32

PL = 64
TX = 32
HALO = 16
NT = 16
COLS = 256
EDGE = 8
HALF = PL * PL // 2
OFFSETS = (
    (2, 2), (2, 1), (2, 3), (1, 2), (3, 2), (1, 1), (1, 3), (3, 1), (3, 3),
    (0, 2), (0, 1), (0, 3), (2, 0), (1, 0), (3, 0),
)
SIDES = tuple((dt, ds) for ds in (-1, 1, 0) for dt in (-1, 0, 1) if (dt, ds) != (0, 0))


def band(shift, delta):
    whole = jnp.right_shift(shift, 2)
    fraction = (shift - 4 * whole).astype(F32) * 0.25
    return jnp.where(
        delta == whole, 1.0 - fraction, jnp.where(delta == whole + 1, fraction, 0.0)
    )


def snake(t):
    z = lax.rem(t, 4)
    return t + lax.rem(t // 4, 2) * (3 - 2 * z)


def kernel(
    ns, vol_ref, shift_ref, corr_ref, reg_ref, tmpl_ref,
    patch, edge_out, edge, raw, across, planes, xw, cur, got, win, turned, mean_out,
    moved, lagged, part, gath,
    local_sem, moved_sem, halo_send, halo_recv, raw_send, raw_recv, rim_send, rim_recv,
    cur_send, cur_recv, win_send, win_recv, mean_send, mean_recv, part_send, part_recv,
):
    t = lax.axis_index("tm")
    s = lax.axis_index("space")
    chunk = snake(t)
    has_lo, has_hi = s > 0, s < ns - 1
    there = {-1: has_lo, 1: has_hi}
    from_side = {-1: has_hi, 1: has_lo}

    def peer(k):
        dx, dz = OFFSETS[k]
        return 4 * lax.rem(t // 4 + dx, 4) + lax.rem(lax.rem(t, 4) + dz, 4)

    def beside(dt):
        return snake(lax.rem(chunk + dt + NT, NT))

    def columns(to):
        return pl.ds(pl.multiple_of(snake(to) * COLS, COLS), COLS)

    def each_peer(body):
        for k in range(NT - 1):
            body(k)

    def remote(src, dst, send, recv, peer):
        return pltpu.make_async_remote_copy(
            src_ref=src, dst_ref=dst, send_sem=send, recv_sem=recv,
            device_id=peer, device_id_type=MESH,
        )

    own = pltpu.make_async_copy(vol_ref.at[0], patch, local_sem)
    own.start()

    barrier = pltpu.get_barrier_semaphore()
    each_peer(
        lambda k: pl.semaphore_signal(
            barrier, inc=1, device_id=(peer(k), s), device_id_type=MESH
        )
    )
    for ds in (-1, 1):

        @pl.when(there[ds])
        def _():
            for dt in (-1, 0, 1):
                pl.semaphore_signal(
                    barrier, inc=1, device_id=(beside(dt), s + ds), device_id_type=MESH
                )

    row = lax.broadcasted_iota(I32, (TX, PL), 0)
    col = lax.broadcasted_iota(I32, (TX, PL), 1)
    which = (col & 15) >> 3
    margin = jnp.where(col < 48, -EDGE, TX) + (col & 7)
    source = [
        jnp.where(col < TX, col, jnp.where(which == half, margin, 2 * PL)) for half in range(2)
    ]
    a = lax.broadcasted_iota(I32, (COLS, COLS), 0)
    b = lax.broadcasted_iota(I32, (COLS, COLS), 1)
    for i in range(2):
        for half in range(2):
            across[i, half] = band(shift_ref[i, 0, 0, 0], row - source[half]).astype(BF16)
        third = band(shift_ref[i, 0, 0, 2], (b & 63) - (a & 63))
        for d in range(4):
            second = band(shift_ref[i, 0, 0, 1], (b >> 6) - (a >> 6) - 4 * (d - 2))
            planes[i, d] = (second * third).astype(BF16)
    xw[0:64] = jnp.zeros((64, COLS), BF16)
    xw[18 * TX : 19 * TX] = jnp.zeros((TX, COLS), BF16)
    for k, ds, at in ((0, -1, 0), (1, 1, 48)):

        @pl.when(jnp.logical_not(there[ds]))
        def _():
            edge[k] = jnp.zeros((HALO, HALF), BF16)
            raw[:, at : at + HALO] = jnp.zeros((NT, HALO, COLS), BF16)
            win[:, :, at : at + HALO] = jnp.zeros((2, 3, HALO, COLS), BF16)

    own.wait()
    for k in range(2):
        wide = patch[HALO * k : HALO * k + HALO].astype(F32)[EDGE * k : EDGE * k + EDGE]
        edge_out[k] = jnp.concatenate([wide[:, :HALF], wide[:, HALF:]], axis=0).astype(BF16)
    pl.semaphore_wait(barrier, NT - 1 + 3 * (has_lo.astype(I32) + has_hi.astype(I32)))

    def halo(ds):
        k = 0 if ds < 0 else 1
        return remote(
            edge_out.at[k], edge.at[1 - k], halo_send.at[k], halo_recv.at[k], (t, s + ds)
        )

    def raw_copy(k):
        to = peer(k)
        return remote(
            patch.at[:, columns(to)], raw.at[t, pl.ds(HALO, TX)],
            raw_send.at[k], raw_recv.at[k], (to, s),
        )

    for ds in (-1, 1):
        pl.when(there[ds])(halo(ds).start)
    each_peer(lambda k: raw_copy(k).start())
    raw[t, HALO : HALO + TX] = patch[:, columns(t)]
    for ds in (-1, 1):
        pl.when(from_side[ds])(halo(ds).wait_recv)

    def warp(i):
        for c in range(NT):
            half, at = c // 8, (c % 8) * COLS
            rows = [patch[:, c * COLS : (c + 1) * COLS]]
            rows += [edge[k, :, at : at + COLS] for k in range(2)]
            xw[(c + 2) * TX : (c + 3) * TX] = jnp.dot(
                across[i, half], jnp.concatenate(rows, axis=0), preferred_element_type=F32
            ).astype(BF16)
        total = jnp.dot(xw[0 : NT * TX], planes[i, 0], preferred_element_type=F32)
        for d in range(1, 4):
            total += jnp.dot(
                xw[d * TX : (d + NT) * TX], planes[i, d], preferred_element_type=F32
            )
        return total.astype(BF16)

    cur[...] = warp(0).reshape(NT, TX, COLS)

    def cur_copy(k):
        to = peer(k)
        return remote(cur.at[snake(to)], got.at[t], cur_send.at[k], cur_recv.at[k], (to, s))

    each_peer(lambda k: cur_copy(k).start())
    got[t] = cur[chunk]

    def win_copy(i, side, act):
        dt, ds = SIDES[side]
        src = {0: HALO, -1: HALO, 1: TX}[ds]
        dst = {0: HALO, -1: 48, 1: 0}[ds]
        rows = TX if ds == 0 else HALO
        copy = remote(
            win.at[i, 1, pl.ds(src, rows)], win.at[i, 1 - dt, pl.ds(dst, rows)],
            win_send.at[i, side], win_recv.at[i, side], (beside(dt), s + ds),
        )
        present = (from_side if act == "wait_recv" else there).get(ds)
        if present is None:
            getattr(copy, act)()
        else:
            pl.when(present)(getattr(copy, act))

    def windows(i, mean):
        win[i, 1, HALO : HALO + TX] = mean.astype(BF16)
        for side in range(8):
            win_copy(i, side, "start")

    each_peer(lambda k: raw_copy(k).wait_recv())
    windows(0, jnp.sum(raw[:, HALO : HALO + TX].astype(F32), axis=0) * (1.0 / NT))

    def rim(ds):
        src, dst = (HALO, 48) if ds < 0 else (TX, 0)
        k = 0 if ds < 0 else 1
        return remote(
            raw.at[:, pl.ds(src, HALO)], raw.at[:, pl.ds(dst, HALO)],
            rim_send.at[k], rim_recv.at[k], (t, s + ds),
        )

    for ds in (-1, 1):
        pl.when(there[ds])(rim(ds).start)

    second_warp = warp(1)
    for c in range(NT):
        moved[0, :, c * COLS : (c + 1) * COLS] = second_warp[c * TX : (c + 1) * TX]
    put_moved = pltpu.make_async_copy(moved, reg_ref, moved_sem)
    put_moved.start()

    each_peer(lambda k: cur_copy(k).wait_recv())
    mean = jnp.sum(got[...].astype(F32), axis=0) * (1.0 / NT)
    windows(1, mean)
    to_place = remote(
        mean_out, tmpl_ref, mean_send, mean_recv, (chunk, s)
    )

    put_mean = pltpu.make_async_copy(mean_out, tmpl_ref, local_sem)
    mean_out[...] = mean
    pl.when(chunk == t)(put_mean.start)
    pl.when(chunk != t)(to_place.start)

    for ds in (-1, 1):
        pl.when(from_side[ds])(rim(ds).wait_recv)
    for j in range(8):
        rows16 = raw[:, 16 * (j // 2) : 16 * (j // 2) + 16].astype(F32)
        eight = rows16[:, 8 * (j % 2) : 8 * (j % 2) + 8].reshape(NT * 8, COLS)
        turned[j] = eight.T.astype(BF16)

    lane = lax.broadcasted_iota(I32, (PL, 128), 1)
    place = lane & 63
    low_half = lane < 64
    step_of = lax.broadcasted_iota(I32, (128, 128), 1) & 7
    owner = lax.broadcasted_iota(I32, (NT, 128), 1) >> 3
    pick = (owner == lax.broadcasted_iota(I32, (NT, 128), 0)).astype(F32)

    def correlate(i):
        blocks = []
        for half in range(6):
            x = win[i, half // 2, :, 128 * (half % 2) : 128 * (half % 2) + 128].astype(F32)
            blocks.append(pltpu.roll(x, 3, 0))

        def both(x):
            return jnp.concatenate([x, x[8:], x[:8]], axis=0).astype(BF16)

        for j3 in range(8):
            lag = j3 - 4
            turn = [pltpu.roll(x, lag % 128, 1) if lag else x for x in blocks]
            other = [pltpu.roll(x, (lag + 64) % 128, 1) for x in blocks]
            if lag > 0:
                inside = place >= lag
            else:
                inside = place < PL + lag
            even = [jnp.where(inside, p, q) for p, q in zip(turn, other)]
            swapped = [jnp.where(inside, q, p) for p, q in zip(turn, other)]
            odd = [
                both(jnp.where(low_half, swapped[h], swapped[h + 1])) for h in range(5)
            ]
            even = [x if h == 0 else both(x) for h, x in enumerate(even)]
            total = jnp.zeros((128, 128), F32)
            for j in range(8):
                rows = slice((j % 2) * PL + 16 * (j // 2), (j % 2) * PL + 16 * (j // 2) + 16)
                stack = []
                for j2 in range(8):
                    off = 8 - j2
                    which = odd if off % 2 else even
                    h = off // 2
                    stack.append(jnp.concatenate([which[h][rows], which[h + 1][rows]], axis=1))
                total += jnp.dot(
                    jnp.concatenate(stack, axis=0), turned[j], preferred_element_type=F32
                )
            for bit in (1, 2, 4):
                total = jnp.where((step_of & bit) != 0, pltpu.roll(total, 128 - bit, 0), total)
            lagged[j3 * 64 : (j3 + 1) * 64] = total.reshape(8, 16, 128)[:, 0:8].reshape(64, 128)
        ordered = jnp.concatenate(
            [
                lagged[pl.ds(j2 * 8 + 7 - j1, 8, stride=64), :]
                for j1 in range(8)
                for j2 in range(8)
            ],
            axis=0,
        )
        sums = lax.dot_general(
            pick, ordered, (((1,), (1,)), ((), ())),
            precision=lax.Precision.HIGHEST, preferred_element_type=F32,
        ) * (1.0 / float(PL) ** 3)
        for k in range(4):
            part[:, 4 * i + k, :] = sums[:, 128 * k : 128 * k + 128]

    for i in range(2):
        for side in range(8):
            win_copy(i, side, "wait_recv")
        correlate(i)

    def part_copy(k):
        to = peer(k)
        return remote(part.at[to], gath.at[t], part_send.at[k], part_recv.at[k], (to, s))

    each_peer(lambda k: part_copy(k).start())
    gath[t] = part[t]
    for ds in (-1, 1):
        pl.when(there[ds])(halo(ds).wait_send)
        pl.when(there[ds])(rim(ds).wait_send)
    each_peer(lambda k: raw_copy(k).wait_send())
    each_peer(lambda k: cur_copy(k).wait_send())
    for i in range(2):
        for side in range(8):
            win_copy(i, side, "wait_send")
    each_peer(lambda k: part_copy(k).wait_recv())
    final = jnp.sum(gath[...], axis=0)
    for i in range(2):
        for k in range(4):
            corr_ref[i, 0, :, 128 * k : 128 * k + 128] = final[4 * i + k : 4 * i + k + 1]
    each_peer(lambda k: part_copy(k).wait_send())
    pl.when(chunk == t)(put_mean.wait)
    pl.when(chunk != t)(to_place.wait)
    put_moved.wait()


def put(*refs):
    *arrays, sems = refs
    copies = [pltpu.make_async_copy(arrays[k], arrays[k + 3], sems.at[k]) for k in range(3)]
    for copy in copies:
        copy.start()
    for copy in copies:
        copy.wait()


def solution(mesh):
    ns = mesh.shape["space"]

    def on_device(volumes, shifts):
        dma = pltpu.SemaphoreType.DMA
        vmem = pltpu.VMEM
        results = pl.pallas_call(
            functools.partial(kernel, ns),
            out_shape=(
                jax.ShapeDtypeStruct((2, 1, 1, 512), F32),
                jax.ShapeDtypeStruct((1, TX, PL * PL), BF16),
                jax.ShapeDtypeStruct((TX, COLS), F32),
            ),
            in_specs=[
                pl.BlockSpec(memory_space=pl.ANY),
                pl.BlockSpec(memory_space=pltpu.SMEM),
            ],
            out_specs=(
                pl.BlockSpec(memory_space=pltpu.VMEM),
                pl.BlockSpec(memory_space=pl.ANY),
                pl.BlockSpec(memory_space=pl.ANY),
            ),
            scratch_shapes=[
                vmem((TX, PL * PL), BF16),
                vmem((2, HALO, HALF), BF16),
                vmem((2, HALO, HALF), BF16),
                vmem((NT, PL, COLS), BF16),
                vmem((2, 2, TX, PL), BF16),
                vmem((2, 4, COLS, COLS), BF16),
                vmem(((NT + 3) * TX, COLS), BF16),
                vmem((NT, TX, COLS), BF16),
                vmem((NT, TX, COLS), BF16),
                vmem((2, 3, PL, COLS), BF16),
                vmem((8, COLS, 128), BF16),
                vmem((TX, COLS), F32),
                vmem((1, TX, PL * PL), BF16),
                vmem((512, 128), F32),
                vmem((NT, 8, 128), F32),
                vmem((NT, 8, 128), F32),
                dma, dma,
                dma((2,)), dma((2,)),
                dma((NT,)), dma((NT,)),
                dma((2,)), dma((2,)),
                dma((NT,)), dma((NT,)),
                dma((2, 8)), dma((2, 8)),
                dma, dma,
                dma((NT,)), dma((NT,)),
            ],
            compiler_params=pltpu.CompilerParams(
                collective_id=0, has_side_effects=True, vmem_limit_bytes=63 * 1024 * 1024
            ),
        )(volumes, shifts.transpose(0, 2, 3, 1))
        return pl.pallas_call(
            put,
            out_shape=tuple(jax.ShapeDtypeStruct(x.shape, x.dtype) for x in results),
            in_specs=[pl.BlockSpec(memory_space=pl.ANY)] * 3,
            out_specs=(pl.BlockSpec(memory_space=pl.ANY),) * 3,
            scratch_shapes=[dma((3,))],
        )(*results)

    return jax.shard_map(
        on_device,
        mesh=mesh,
        in_specs=(P("tm", "space", None), P(None, None, "tm", "space")),
        out_specs=(P(None, "tm", "space", None), P("tm", "space", None), P("space", "tm")),
        check_vma=False,
    )
```

```python
import functools

import jax
import jax.numpy as jnp
from jax import lax
from jax.experimental import pallas as pl
from jax.experimental.pallas import tpu as pltpu
from jax.sharding import PartitionSpec as P

MESH = pl.DeviceIdType.MESH
F32, BF16, I32 = jnp.float32, jnp.bfloat16, jnp.int32

PL = 64
TX = 32
HALO = 16
NT = 16
COLS = 256
EDGE = 8
HALF = PL * PL // 2
OFFSETS = (
    (2, 2), (2, 1), (2, 3), (1, 2), (3, 2), (1, 1), (1, 3), (3, 1), (3, 3),
    (0, 2), (0, 1), (0, 3), (2, 0), (1, 0), (3, 0),
)
SIDES = tuple((dt, ds) for ds in (-1, 1, 0) for dt in (-1, 0, 1) if (dt, ds) != (0, 0))


def band(shift, delta):
    whole = jnp.right_shift(shift, 2)
    fraction = (shift - 4 * whole).astype(F32) * 0.25
    return jnp.where(
        delta == whole, 1.0 - fraction, jnp.where(delta == whole + 1, fraction, 0.0)
    )


def snake(t):
    z = lax.rem(t, 4)
    return t + lax.rem(t // 4, 2) * (3 - 2 * z)


def kernel(
    ns, vol_ref, shift_ref, corr_ref, reg_ref, tmpl_ref,
    patch, edge_out, edge, raw, across, planes, xw, cur, got, win, turned, mean_out,
    moved, lagged, part, gath,
    local_sem, moved_sem, halo_send, halo_recv, raw_send, raw_recv, rim_send, rim_recv,
    cur_send, cur_recv, win_send, win_recv, mean_send, mean_recv, part_send, part_recv,
):
    t = lax.axis_index("tm")
    s = lax.axis_index("space")
    chunk = snake(t)
    has_lo, has_hi = s > 0, s < ns - 1
    there = {-1: has_lo, 1: has_hi}
    from_side = {-1: has_hi, 1: has_lo}

    def peer(k):
        dx, dz = OFFSETS[k]
        return 4 * lax.rem(t // 4 + dx, 4) + lax.rem(lax.rem(t, 4) + dz, 4)

    def beside(dt):
        return snake(lax.rem(chunk + dt + NT, NT))

    def columns(to):
        return pl.ds(pl.multiple_of(snake(to) * COLS, COLS), COLS)

    def each_peer(body):
        for k in range(NT - 1):
            body(k)

    def remote(src, dst, send, recv, peer):
        return pltpu.make_async_remote_copy(
            src_ref=src, dst_ref=dst, send_sem=send, recv_sem=recv,
            device_id=peer, device_id_type=MESH,
        )

    own = pltpu.make_async_copy(vol_ref.at[0], patch, local_sem)
    own.start()

    barrier = pltpu.get_barrier_semaphore()
    each_peer(
        lambda k: pl.semaphore_signal(
            barrier, inc=1, device_id=(peer(k), s), device_id_type=MESH
        )
    )
    for ds in (-1, 1):

        @pl.when(there[ds])
        def _():
            for dt in (-1, 0, 1):
                pl.semaphore_signal(
                    barrier, inc=1, device_id=(beside(dt), s + ds), device_id_type=MESH
                )

    row = lax.broadcasted_iota(I32, (TX, PL), 0)
    col = lax.broadcasted_iota(I32, (TX, PL), 1)
    which = (col & 15) >> 3
    margin = jnp.where(col < 48, -EDGE, TX) + (col & 7)
    source = [
        jnp.where(col < TX, col, jnp.where(which == half, margin, 2 * PL)) for half in range(2)
    ]
    a = lax.broadcasted_iota(I32, (COLS, COLS), 0)
    b = lax.broadcasted_iota(I32, (COLS, COLS), 1)
    for i in range(2):
        for half in range(2):
            across[i, half] = band(shift_ref[i, 0, 0, 0], row - source[half]).astype(BF16)
        third = band(shift_ref[i, 0, 0, 2], (b & 63) - (a & 63))
        for d in range(4):
            second = band(shift_ref[i, 0, 0, 1], (b >> 6) - (a >> 6) - 4 * (d - 2))
            planes[i, d] = (second * third).astype(BF16)
    xw[0:64] = jnp.zeros((64, COLS), BF16)
    xw[18 * TX : 19 * TX] = jnp.zeros((TX, COLS), BF16)
    for k, ds, at in ((0, -1, 0), (1, 1, 48)):

        @pl.when(jnp.logical_not(there[ds]))
        def _():
            edge[k] = jnp.zeros((HALO, HALF), BF16)
            raw[:, at : at + HALO] = jnp.zeros((NT, HALO, COLS), BF16)
            win[:, :, at : at + HALO] = jnp.zeros((2, 3, HALO, COLS), BF16)

    own.wait()
    for k in range(2):
        wide = patch[HALO * k : HALO * k + HALO].astype(F32)[EDGE * k : EDGE * k + EDGE]
        edge_out[k] = jnp.concatenate([wide[:, :HALF], wide[:, HALF:]], axis=0).astype(BF16)
    pl.semaphore_wait(barrier, NT - 1 + 3 * (has_lo.astype(I32) + has_hi.astype(I32)))

    def halo(ds):
        k = 0 if ds < 0 else 1
        return remote(
            edge_out.at[k], edge.at[1 - k], halo_send.at[k], halo_recv.at[k], (t, s + ds)
        )

    def raw_copy(k):
        to = peer(k)
        return remote(
            patch.at[:, columns(to)], raw.at[t, pl.ds(HALO, TX)],
            raw_send.at[k], raw_recv.at[k], (to, s),
        )

    for ds in (-1, 1):
        pl.when(there[ds])(halo(ds).start)
    each_peer(lambda k: raw_copy(k).start())
    raw[t, HALO : HALO + TX] = patch[:, columns(t)]
    for ds in (-1, 1):
        pl.when(from_side[ds])(halo(ds).wait_recv)

    def warp(i):
        for c in range(NT):
            half, at = c // 8, (c % 8) * COLS
            rows = [patch[:, c * COLS : (c + 1) * COLS]]
            rows += [edge[k, :, at : at + COLS] for k in range(2)]
            xw[(c + 2) * TX : (c + 3) * TX] = jnp.dot(
                across[i, half], jnp.concatenate(rows, axis=0), preferred_element_type=F32
            ).astype(BF16)
        total = jnp.dot(xw[0 : NT * TX], planes[i, 0], preferred_element_type=F32)
        for d in range(1, 4):
            total += jnp.dot(
                xw[d * TX : (d + NT) * TX], planes[i, d], preferred_element_type=F32
            )
        return total.astype(BF16)

    cur[...] = warp(0).reshape(NT, TX, COLS)

    def cur_copy(k):
        to = peer(k)
        return remote(cur.at[snake(to)], got.at[t], cur_send.at[k], cur_recv.at[k], (to, s))

    each_peer(lambda k: cur_copy(k).start())
    got[t] = cur[chunk]

    def win_copy(i, side, act):
        dt, ds = SIDES[side]
        src = {0: HALO, -1: HALO, 1: TX}[ds]
        dst = {0: HALO, -1: 48, 1: 0}[ds]
        rows = TX if ds == 0 else HALO
        copy = remote(
            win.at[i, 1, pl.ds(src, rows)], win.at[i, 1 - dt, pl.ds(dst, rows)],
            win_send.at[i, side], win_recv.at[i, side], (beside(dt), s + ds),
        )
        present = (from_side if act == "wait_recv" else there).get(ds)
        if present is None:
            getattr(copy, act)()
        else:
            pl.when(present)(getattr(copy, act))

    def windows(i, mean):
        win[i, 1, HALO : HALO + TX] = mean.astype(BF16)
        for side in range(8):
            win_copy(i, side, "start")

    each_peer(lambda k: raw_copy(k).wait_recv())
    windows(0, jnp.sum(raw[:, HALO : HALO + TX].astype(F32), axis=0) * (1.0 / NT))

    def rim(ds):
        src, dst = (HALO, 48) if ds < 0 else (TX, 0)
        k = 0 if ds < 0 else 1
        return remote(
            raw.at[:, pl.ds(src, HALO)], raw.at[:, pl.ds(dst, HALO)],
            rim_send.at[k], rim_recv.at[k], (t, s + ds),
        )

    for ds in (-1, 1):
        pl.when(there[ds])(rim(ds).start)

    second_warp = warp(1)
    for c in range(NT):
        moved[0, :, c * COLS : (c + 1) * COLS] = second_warp[c * TX : (c + 1) * TX]
    put_moved = pltpu.make_async_copy(moved, reg_ref, moved_sem)
    put_moved.start()

    each_peer(lambda k: cur_copy(k).wait_recv())
    mean = jnp.sum(got[...].astype(F32), axis=0) * (1.0 / NT)
    windows(1, mean)
    to_place = remote(
        mean_out, tmpl_ref, mean_send, mean_recv, (chunk, s)
    )

    put_mean = pltpu.make_async_copy(mean_out, tmpl_ref, local_sem)
    mean_out[...] = mean
    pl.when(chunk == t)(put_mean.start)
    pl.when(chunk != t)(to_place.start)

    for ds in (-1, 1):
        pl.when(from_side[ds])(rim(ds).wait_recv)
    for j in range(8):
        rows16 = raw[:, 16 * (j // 2) : 16 * (j // 2) + 16].astype(F32)
        eight = rows16[:, 8 * (j % 2) : 8 * (j % 2) + 8].reshape(NT * 8, COLS)
        turned[j] = eight.T.astype(BF16)

    lane = lax.broadcasted_iota(I32, (PL, 128), 1)
    place = lane & 63
    low_half = lane < 64
    step_of = lax.broadcasted_iota(I32, (128, 128), 1) & 7
    owner = lax.broadcasted_iota(I32, (NT, 128), 1) >> 3
    pick = (owner == lax.broadcasted_iota(I32, (NT, 128), 0)).astype(F32)

    def correlate(i):
        blocks = []
        for half in range(6):
            x = win[i, half // 2, :, 128 * (half % 2) : 128 * (half % 2) + 128].astype(F32)
            blocks.append(pltpu.roll(x, 3, 0))

        def both(x):
            return jnp.concatenate([x, x[8:], x[:8]], axis=0).astype(BF16)

        for j3 in range(8):
            lag = j3 - 4
            turn = [pltpu.roll(x, lag % 128, 1) if lag else x for x in blocks]
            other = [pltpu.roll(x, (lag + 64) % 128, 1) for x in blocks]
            if lag > 0:
                inside = place >= lag
            else:
                inside = place < PL + lag
            even = [jnp.where(inside, p, q) for p, q in zip(turn, other)]
            swapped = [jnp.where(inside, q, p) for p, q in zip(turn, other)]
            odd = [
                both(jnp.where(low_half, swapped[h], swapped[h + 1])) for h in range(5)
            ]
            even = [x if h == 0 else both(x) for h, x in enumerate(even)]
            total = jnp.zeros((128, 128), F32)
            for j in range(8):
                rows = slice((j % 2) * PL + 16 * (j // 2), (j % 2) * PL + 16 * (j // 2) + 16)
                stack = []
                for j2 in range(8):
                    off = 8 - j2
                    which = odd if off % 2 else even
                    h = off // 2
                    stack.append(jnp.concatenate([which[h][rows], which[h + 1][rows]], axis=1))
                total += jnp.dot(
                    jnp.concatenate(stack, axis=0), turned[j], preferred_element_type=F32
                )
            for bit in (1, 2, 4):
                total = jnp.where((step_of & bit) != 0, pltpu.roll(total, 128 - bit, 0), total)
            lagged[j3 * 64 : (j3 + 1) * 64] = total.reshape(8, 16, 128)[:, 0:8].reshape(64, 128)
        ordered = jnp.concatenate(
            [
                lagged[pl.ds(j2 * 8 + 7 - j1, 8, stride=64), :]
                for j1 in range(8)
                for j2 in range(8)
            ],
            axis=0,
        )
        sums = lax.dot_general(
            pick, ordered, (((1,), (1,)), ((), ())),
            precision=lax.Precision.HIGHEST, preferred_element_type=F32,
        ) * (1.0 / float(PL) ** 3)
        for k in range(4):
            part[:, 4 * i + k, :] = sums[:, 128 * k : 128 * k + 128]

    for i in range(2):
        for side in range(8):
            win_copy(i, side, "wait_recv")
        correlate(i)

    def part_copy(k):
        to = peer(k)
        return remote(part.at[to], gath.at[t], part_send.at[k], part_recv.at[k], (to, s))

    each_peer(lambda k: part_copy(k).start())
    gath[t] = part[t]
    for ds in (-1, 1):
        pl.when(there[ds])(halo(ds).wait_send)
        pl.when(there[ds])(rim(ds).wait_send)
    each_peer(lambda k: raw_copy(k).wait_send())
    each_peer(lambda k: cur_copy(k).wait_send())
    for i in range(2):
        for side in range(8):
            win_copy(i, side, "wait_send")
    each_peer(lambda k: part_copy(k).wait_recv())
    final = jnp.sum(gath[...], axis=0)
    for i in range(2):
        for k in range(4):
            corr_ref[i, 0, :, 128 * k : 128 * k + 128] = final[4 * i + k : 4 * i + k + 1]
    each_peer(lambda k: part_copy(k).wait_send())
    pl.when(chunk == t)(put_mean.wait)
    pl.when(chunk != t)(to_place.wait)
    put_moved.wait()


def put(*refs):
    *arrays, sems = refs
    copies = [pltpu.make_async_copy(arrays[k], arrays[k + 3], sems.at[k]) for k in range(3)]
    for copy in copies:
        copy.start()
    for copy in copies:
        copy.wait()


def solution(mesh):
    ns = mesh.shape["space"]

    def on_device(volumes, shifts):
        dma = pltpu.SemaphoreType.DMA
        vmem = pltpu.VMEM
        results = pl.pallas_call(
            functools.partial(kernel, ns),
            out_shape=(
                jax.ShapeDtypeStruct((2, 1, 1, 512), F32),
                jax.ShapeDtypeStruct((1, TX, PL * PL), BF16),
                jax.ShapeDtypeStruct((TX, COLS), F32),
            ),
            in_specs=[
                pl.BlockSpec(memory_space=pl.ANY),
                pl.BlockSpec(memory_space=pltpu.SMEM),
            ],
            out_specs=(
                pl.BlockSpec(memory_space=pltpu.VMEM),
                pl.BlockSpec(memory_space=pl.ANY),
                pl.BlockSpec(memory_space=pl.ANY),
            ),
            scratch_shapes=[
                vmem((TX, PL * PL), BF16),
                vmem((2, HALO, HALF), BF16),
                vmem((2, HALO, HALF), BF16),
                vmem((NT, PL, COLS), BF16),
                vmem((2, 2, TX, PL), BF16),
                vmem((2, 4, COLS, COLS), BF16),
                vmem(((NT + 3) * TX, COLS), BF16),
                vmem((NT, TX, COLS), BF16),
                vmem((NT, TX, COLS), BF16),
                vmem((2, 3, PL, COLS), BF16),
                vmem((8, COLS, 128), BF16),
                vmem((TX, COLS), F32),
                vmem((1, TX, PL * PL), BF16),
                vmem((512, 128), F32),
                vmem((NT, 8, 128), F32),
                vmem((NT, 8, 128), F32),
                dma, dma,
                dma((2,)), dma((2,)),
                dma((NT,)), dma((NT,)),
                dma((2,)), dma((2,)),
                dma((NT,)), dma((NT,)),
                dma((2, 8)), dma((2, 8)),
                dma, dma,
                dma((NT,)), dma((NT,)),
            ],
            compiler_params=pltpu.CompilerParams(
                collective_id=0, has_side_effects=True, vmem_limit_bytes=40 * 1024 * 1024
            ),
        )(volumes, shifts.transpose(0, 2, 3, 1))
        return pl.pallas_call(
            put,
            out_shape=tuple(jax.ShapeDtypeStruct(x.shape, x.dtype) for x in results),
            in_specs=[pl.BlockSpec(memory_space=pl.ANY)] * 3,
            out_specs=(pl.BlockSpec(memory_space=pl.ANY),) * 3,
            scratch_shapes=[dma((3,))],
            compiler_params=pltpu.CompilerParams(vmem_limit_bytes=1024 * 1024),
        )(*results)

    return jax.shard_map(
        on_device,
        mesh=mesh,
        in_specs=(P("tm", "space", None), P(None, None, "tm", "space")),
        out_specs=(P(None, "tm", "space", None), P("tm", "space", None), P("space", "tm")),
        check_vma=False,
    )
```

```python
import functools

import jax
import jax.numpy as jnp
from jax import lax
from jax.experimental import pallas as pl
from jax.experimental.pallas import tpu as pltpu
from jax.sharding import PartitionSpec as P

MESH = pl.DeviceIdType.MESH
F32, BF16, I32 = jnp.float32, jnp.bfloat16, jnp.int32

PL = 64
TX = 32
HALO = 16
NT = 16
COLS = 256
EDGE = 8
HALF = PL * PL // 2
OFFSETS = (
    (2, 2), (2, 1), (2, 3), (1, 2), (3, 2), (1, 1), (1, 3), (3, 1), (3, 3),
    (0, 2), (0, 1), (0, 3), (2, 0), (1, 0), (3, 0),
)
SIDES = tuple((dt, ds) for ds in (-1, 1, 0) for dt in (-1, 0, 1) if (dt, ds) != (0, 0))


def band(shift, delta):
    whole = jnp.right_shift(shift, 2)
    fraction = (shift - 4 * whole).astype(F32) * 0.25
    return jnp.where(
        delta == whole, 1.0 - fraction, jnp.where(delta == whole + 1, fraction, 0.0)
    )


def snake(t):
    z = lax.rem(t, 4)
    return t + lax.rem(t // 4, 2) * (3 - 2 * z)


def kernel(
    ns, vol_ref, shift_ref, corr_ref, reg_ref, tmpl_ref,
    edge_out, edge, raw, across, planes, xw, cur, got, win, turned, mean_out,
    lagged, part, gath,
    local_sem, halo_send, halo_recv, raw_send, raw_recv, rim_send, rim_recv,
    cur_send, cur_recv, win_send, win_recv, mean_send, mean_recv, part_send, part_recv,
):
    t = lax.axis_index("tm")
    s = lax.axis_index("space")
    chunk = snake(t)
    has_lo, has_hi = s > 0, s < ns - 1
    there = {-1: has_lo, 1: has_hi}
    from_side = {-1: has_hi, 1: has_lo}

    def peer(k):
        dx, dz = OFFSETS[k]
        return 4 * lax.rem(t // 4 + dx, 4) + lax.rem(lax.rem(t, 4) + dz, 4)

    def beside(dt):
        return snake(lax.rem(chunk + dt + NT, NT))

    def columns(to):
        return pl.ds(pl.multiple_of(snake(to) * COLS, COLS), COLS)

    def each_peer(body):
        for k in range(NT - 1):
            body(k)

    def remote(src, dst, send, recv, peer):
        return pltpu.make_async_remote_copy(
            src_ref=src, dst_ref=dst, send_sem=send, recv_sem=recv,
            device_id=peer, device_id_type=MESH,
        )

    barrier = pltpu.get_barrier_semaphore()
    each_peer(
        lambda k: pl.semaphore_signal(
            barrier, inc=1, device_id=(peer(k), s), device_id_type=MESH
        )
    )
    for ds in (-1, 1):

        @pl.when(there[ds])
        def _():
            for dt in (-1, 0, 1):
                pl.semaphore_signal(
                    barrier, inc=1, device_id=(beside(dt), s + ds), device_id_type=MESH
                )

    for k in range(2):
        wide = vol_ref[0, HALO * k : HALO * k + HALO].astype(F32)[EDGE * k : EDGE * k + EDGE]
        edge_out[k] = jnp.concatenate([wide[:, :HALF], wide[:, HALF:]], axis=0).astype(BF16)
    pl.semaphore_wait(barrier, NT - 1 + 3 * (has_lo.astype(I32) + has_hi.astype(I32)))

    def halo(ds):
        k = 0 if ds < 0 else 1
        return remote(
            edge_out.at[k], edge.at[1 - k], halo_send.at[k], halo_recv.at[k], (t, s + ds)
        )

    def raw_copy(k):
        to = peer(k)
        return remote(
            vol_ref.at[0, :, columns(to)], raw.at[t, pl.ds(HALO, TX)],
            raw_send.at[k], raw_recv.at[k], (to, s),
        )

    for ds in (-1, 1):
        pl.when(there[ds])(halo(ds).start)
    each_peer(lambda k: raw_copy(k).start())
    raw[t, HALO : HALO + TX] = vol_ref[0, :, columns(t)]

    row = lax.broadcasted_iota(I32, (TX, PL), 0)
    col = lax.broadcasted_iota(I32, (TX, PL), 1)
    which = (col & 15) >> 3
    margin = jnp.where(col < 48, -EDGE, TX) + (col & 7)
    source = [
        jnp.where(col < TX, col, jnp.where(which == half, margin, 2 * PL)) for half in range(2)
    ]
    a = lax.broadcasted_iota(I32, (COLS, COLS), 0)
    b = lax.broadcasted_iota(I32, (COLS, COLS), 1)
    for i in range(2):
        for half in range(2):
            across[i, half] = band(shift_ref[i, 0, 0, 0], row - source[half]).astype(BF16)
        third = band(shift_ref[i, 0, 0, 2], (b & 63) - (a & 63))
        for d in range(4):
            second = band(shift_ref[i, 0, 0, 1], (b >> 6) - (a >> 6) - 4 * (d - 2))
            planes[i, d] = (second * third).astype(BF16)
    xw[0:64] = jnp.zeros((64, COLS), BF16)
    xw[18 * TX : 19 * TX] = jnp.zeros((TX, COLS), BF16)
    for k, ds, at in ((0, -1, 0), (1, 1, 48)):

        @pl.when(jnp.logical_not(there[ds]))
        def _():
            edge[k] = jnp.zeros((HALO, HALF), BF16)
            raw[:, at : at + HALO] = jnp.zeros((NT, HALO, COLS), BF16)
            win[:, :, at : at + HALO] = jnp.zeros((2, 3, HALO, COLS), BF16)
    for ds in (-1, 1):
        pl.when(from_side[ds])(halo(ds).wait_recv)

    def warp(i):
        for c in range(NT):
            half, at = c // 8, (c % 8) * COLS
            rows = [vol_ref[0, :, c * COLS : (c + 1) * COLS]]
            rows += [edge[k, :, at : at + COLS] for k in range(2)]
            xw[(c + 2) * TX : (c + 3) * TX] = jnp.dot(
                across[i, half], jnp.concatenate(rows, axis=0), preferred_element_type=F32
            ).astype(BF16)
        total = jnp.dot(xw[0 : NT * TX], planes[i, 0], preferred_element_type=F32)
        for d in range(1, 4):
            total += jnp.dot(
                xw[d * TX : (d + NT) * TX], planes[i, d], preferred_element_type=F32
            )
        return total.astype(BF16)

    cur[...] = warp(0).reshape(NT, TX, COLS)

    def cur_copy(k):
        to = peer(k)
        return remote(cur.at[snake(to)], got.at[t], cur_send.at[k], cur_recv.at[k], (to, s))

    each_peer(lambda k: cur_copy(k).start())
    got[t] = cur[chunk]

    def win_copy(i, side, act):
        dt, ds = SIDES[side]
        src = {0: HALO, -1: HALO, 1: TX}[ds]
        dst = {0: HALO, -1: 48, 1: 0}[ds]
        rows = TX if ds == 0 else HALO
        copy = remote(
            win.at[i, 1, pl.ds(src, rows)], win.at[i, 1 - dt, pl.ds(dst, rows)],
            win_send.at[i, side], win_recv.at[i, side], (beside(dt), s + ds),
        )
        present = (from_side if act == "wait_recv" else there).get(ds)
        if present is None:
            getattr(copy, act)()
        else:
            pl.when(present)(getattr(copy, act))

    def windows(i, mean):
        win[i, 1, HALO : HALO + TX] = mean.astype(BF16)
        for side in range(8):
            win_copy(i, side, "start")

    each_peer(lambda k: raw_copy(k).wait_recv())
    windows(0, jnp.sum(raw[:, HALO : HALO + TX].astype(F32), axis=0) * (1.0 / NT))

    def rim(ds):
        src, dst = (HALO, 48) if ds < 0 else (TX, 0)
        k = 0 if ds < 0 else 1
        return remote(
            raw.at[:, pl.ds(src, HALO)], raw.at[:, pl.ds(dst, HALO)],
            rim_send.at[k], rim_recv.at[k], (t, s + ds),
        )

    for ds in (-1, 1):
        pl.when(there[ds])(rim(ds).start)

    second_warp = warp(1)
    for c in range(NT):
        reg_ref[0, :, c * COLS : (c + 1) * COLS] = second_warp[c * TX : (c + 1) * TX]

    each_peer(lambda k: cur_copy(k).wait_recv())
    mean = jnp.sum(got[...].astype(F32), axis=0) * (1.0 / NT)
    windows(1, mean)
    to_place = remote(
        mean_out, tmpl_ref, mean_send, mean_recv, (chunk, s)
    )

    mean_out[...] = mean
    put_mean = pltpu.make_async_copy(mean_out, tmpl_ref, local_sem)
    pl.when(chunk == t)(put_mean.start)
    pl.when(chunk != t)(to_place.start)

    for ds in (-1, 1):
        pl.when(from_side[ds])(rim(ds).wait_recv)
    for j in range(8):
        rows16 = raw[:, 16 * (j // 2) : 16 * (j // 2) + 16].astype(F32)
        eight = rows16[:, 8 * (j % 2) : 8 * (j % 2) + 8].reshape(NT * 8, COLS)
        turned[j] = eight.T.astype(BF16)

    lane = lax.broadcasted_iota(I32, (PL, 128), 1)
    place = lane & 63
    low_half = lane < 64
    step_of = lax.broadcasted_iota(I32, (128, 128), 1) & 7
    owner = lax.broadcasted_iota(I32, (NT, 128), 1) >> 3
    pick = (owner == lax.broadcasted_iota(I32, (NT, 128), 0)).astype(BF16)

    def correlate(i):
        blocks = []
        for half in range(6):
            x = win[i, half // 2, :, 128 * (half % 2) : 128 * (half % 2) + 128].astype(F32)
            blocks.append(pltpu.roll(x, 3, 0))

        def both(x):
            return jnp.concatenate([x, x[8:], x[:8]], axis=0).astype(BF16)

        for j3 in range(8):
            lag = j3 - 4
            turn = [pltpu.roll(x, lag % 128, 1) if lag else x for x in blocks]
            other = [pltpu.roll(x, (lag + 64) % 128, 1) for x in blocks]
            if lag > 0:
                inside = place >= lag
            else:
                inside = place < PL + lag
            even = [jnp.where(inside, p, q) for p, q in zip(turn, other)]
            swapped = [jnp.where(inside, q, p) for p, q in zip(turn, other)]
            odd = [
                both(jnp.where(low_half, swapped[h], swapped[h + 1])) for h in range(5)
            ]
            even = [x if h == 0 else both(x) for h, x in enumerate(even)]
            total = jnp.zeros((128, 128), F32)
            for j in range(8):
                rows = slice((j % 2) * PL + 16 * (j // 2), (j % 2) * PL + 16 * (j // 2) + 16)
                stack = []
                for j2 in range(8):
                    off = 8 - j2
                    which = odd if off % 2 else even
                    h = off // 2
                    stack.append(jnp.concatenate([which[h][rows], which[h + 1][rows]], axis=1))
                total += jnp.dot(
                    jnp.concatenate(stack, axis=0), turned[j], preferred_element_type=F32
                )
            for bit in (1, 2, 4):
                total = jnp.where((step_of & bit) != 0, pltpu.roll(total, 128 - bit, 0), total)
            lagged[j3 * 64 : (j3 + 1) * 64] = total.reshape(8, 16, 128)[:, 0:8].reshape(64, 128)
        ordered = jnp.concatenate(
            [
                lagged[pl.ds(j2 * 8 + 7 - j1, 8, stride=64), :]
                for j1 in range(8)
                for j2 in range(8)
            ],
            axis=0,
        )
        upper = ordered.astype(BF16)
        lower = (ordered - upper.astype(F32)).astype(BF16)
        sums = sum(
            lax.dot_general(
                pick, x, (((1,), (1,)), ((), ())), preferred_element_type=F32
            )
            for x in (upper, lower)
        ) * (1.0 / float(PL) ** 3)
        for k in range(4):
            part[:, 4 * i + k, :] = sums[:, 128 * k : 128 * k + 128]

    for i in range(2):
        for side in range(8):
            win_copy(i, side, "wait_recv")
        correlate(i)

    def part_copy(k):
        to = peer(k)
        return remote(part.at[to], gath.at[t], part_send.at[k], part_recv.at[k], (to, s))

    each_peer(lambda k: part_copy(k).start())
    gath[t] = part[t]
    for ds in (-1, 1):
        pl.when(there[ds])(halo(ds).wait_send)
        pl.when(there[ds])(rim(ds).wait_send)
    each_peer(lambda k: raw_copy(k).wait_send())
    each_peer(lambda k: cur_copy(k).wait_send())
    for i in range(2):
        for side in range(8):
            win_copy(i, side, "wait_send")
    each_peer(lambda k: part_copy(k).wait_recv())
    final = jnp.sum(gath[...], axis=0)
    for i in range(2):
        for k in range(4):
            corr_ref[i, 0, :, 128 * k : 128 * k + 128] = final[4 * i + k : 4 * i + k + 1]
    each_peer(lambda k: part_copy(k).wait_send())
    pl.when(chunk == t)(put_mean.wait)
    pl.when(chunk != t)(to_place.wait)


def put(*refs):
    *arrays, sems = refs
    copies = [pltpu.make_async_copy(arrays[k], arrays[k + 3], sems.at[k]) for k in range(3)]
    for copy in copies:
        copy.start()
    for copy in copies:
        copy.wait()


def solution(mesh):
    ns = mesh.shape["space"]

    def on_device(volumes, shifts):
        dma = pltpu.SemaphoreType.DMA
        vmem = pltpu.VMEM
        results = pl.pallas_call(
            functools.partial(kernel, ns),
            out_shape=(
                jax.ShapeDtypeStruct((2, 1, 1, 512), F32),
                jax.ShapeDtypeStruct((1, TX, PL * PL), BF16),
                jax.ShapeDtypeStruct((TX, COLS), F32),
            ),
            in_specs=[
                pl.BlockSpec(memory_space=pltpu.VMEM),
                pl.BlockSpec(memory_space=pltpu.SMEM),
            ],
            out_specs=(
                pl.BlockSpec(memory_space=pltpu.VMEM),
                pl.BlockSpec(memory_space=pltpu.VMEM),
                pl.BlockSpec(memory_space=pltpu.VMEM),
            ),
            scratch_shapes=[
                vmem((2, HALO, HALF), BF16),
                vmem((2, HALO, HALF), BF16),
                vmem((NT, PL, COLS), BF16),
                vmem((2, 2, TX, PL), BF16),
                vmem((2, 4, COLS, COLS), BF16),
                vmem(((NT + 3) * TX, COLS), BF16),
                vmem((NT, TX, COLS), BF16),
                vmem((NT, TX, COLS), BF16),
                vmem((2, 3, PL, COLS), BF16),
                vmem((8, COLS, 128), BF16),
                vmem((TX, COLS), F32),
                vmem((512, 128), F32),
                vmem((NT, 8, 128), F32),
                vmem((NT, 8, 128), F32),
                dma,
                dma((2,)), dma((2,)),
                dma((NT,)), dma((NT,)),
                dma((2,)), dma((2,)),
                dma((NT,)), dma((NT,)),
                dma((2, 8)), dma((2, 8)),
                dma, dma,
                dma((NT,)), dma((NT,)),
            ],
            compiler_params=pltpu.CompilerParams(
                collective_id=0, has_side_effects=True, vmem_limit_bytes=40 * 1024 * 1024
            ),
        )(volumes, shifts.transpose(0, 2, 3, 1))
        return pl.pallas_call(
            put,
            out_shape=tuple(jax.ShapeDtypeStruct(x.shape, x.dtype) for x in results),
            in_specs=[pl.BlockSpec(memory_space=pl.ANY)] * 3,
            out_specs=(pl.BlockSpec(memory_space=pl.ANY),) * 3,
            scratch_shapes=[dma((3,))],
            compiler_params=pltpu.CompilerParams(vmem_limit_bytes=1024 * 1024),
        )(*results)

    return jax.shard_map(
        on_device,
        mesh=mesh,
        in_specs=(P("tm", "space", None), P(None, None, "tm", "space")),
        out_specs=(P(None, "tm", "space", None), P("tm", "space", None), P("space", "tm")),
        check_vma=False,
    )
```

```python
import functools

import jax
import jax.numpy as jnp
from jax import lax
from jax.experimental import pallas as pl
from jax.experimental.pallas import tpu as pltpu
from jax.sharding import PartitionSpec as P

MESH = pl.DeviceIdType.MESH
F32, BF16, I32 = jnp.float32, jnp.bfloat16, jnp.int32

PL = 64
TX = 32
HALO = 16
NT = 16
COLS = 256
EDGE = 8
HALF = PL * PL // 2
OFFSETS = (
    (2, 2), (2, 1), (2, 3), (1, 2), (3, 2), (1, 1), (1, 3), (3, 1), (3, 3),
    (0, 2), (0, 1), (0, 3), (2, 0), (1, 0), (3, 0),
)
SIDES = tuple((dt, ds) for ds in (-1, 1, 0) for dt in (-1, 0, 1) if (dt, ds) != (0, 0))


def band(shift, delta):
    whole = jnp.right_shift(shift, 2)
    fraction = (shift - 4 * whole).astype(F32) * 0.25
    return jnp.where(
        delta == whole, 1.0 - fraction, jnp.where(delta == whole + 1, fraction, 0.0)
    )


def snake(t):
    z = lax.rem(t, 4)
    return t + lax.rem(t // 4, 2) * (3 - 2 * z)


def kernel(
    ns, vol_ref, shift_ref, corr_ref, reg_ref, tmpl_ref,
    edge_out, edge, raw, across, planes, xw, cur, got, sums, shares, win, turned, mean_out,
    lagged, part, gath,
    local_sem, halo_send, halo_recv, raw_send, raw_recv, rim_send, rim_recv,
    cur_send, cur_recv, share_send, share_recv, win_send, win_recv, mean_send, mean_recv, part_send, part_recv,
):
    t = lax.axis_index("tm")
    s = lax.axis_index("space")
    chunk = snake(t)
    has_lo, has_hi = s > 0, s < ns - 1
    there = {-1: has_lo, 1: has_hi}
    from_side = {-1: has_hi, 1: has_lo}

    def peer(k):
        dx, dz = OFFSETS[k]
        return 4 * lax.rem(t // 4 + dx, 4) + lax.rem(lax.rem(t, 4) + dz, 4)

    def beside(dt):
        return snake(lax.rem(chunk + dt + NT, NT))

    x, z = t // 4, lax.rem(t, 4)

    def columns(to):
        return pl.ds(pl.multiple_of(snake(to) * COLS, COLS), COLS)

    def each_peer(body):
        for k in range(NT - 1):
            body(k)

    def remote(src, dst, send, recv, peer):
        return pltpu.make_async_remote_copy(
            src_ref=src, dst_ref=dst, send_sem=send, recv_sem=recv,
            device_id=peer, device_id_type=MESH,
        )

    barrier = pltpu.get_barrier_semaphore()
    each_peer(
        lambda k: pl.semaphore_signal(
            barrier, inc=1, device_id=(peer(k), s), device_id_type=MESH
        )
    )
    for ds in (-1, 1):

        @pl.when(there[ds])
        def _():
            for dt in (-1, 0, 1):
                pl.semaphore_signal(
                    barrier, inc=1, device_id=(beside(dt), s + ds), device_id_type=MESH
                )

    for k in range(2):
        wide = vol_ref[0, HALO * k : HALO * k + HALO].astype(F32)[EDGE * k : EDGE * k + EDGE]
        edge_out[k] = jnp.concatenate([wide[:, :HALF], wide[:, HALF:]], axis=0).astype(BF16)
    pl.semaphore_wait(barrier, NT - 1 + 3 * (has_lo.astype(I32) + has_hi.astype(I32)))

    def halo(ds):
        k = 0 if ds < 0 else 1
        return remote(
            edge_out.at[k], edge.at[1 - k], halo_send.at[k], halo_recv.at[k], (t, s + ds)
        )

    def raw_copy(k):
        to = peer(k)
        return remote(
            vol_ref.at[0, :, columns(to)], raw.at[t, pl.ds(HALO, TX)],
            raw_send.at[k], raw_recv.at[k], (to, s),
        )

    for ds in (-1, 1):
        pl.when(there[ds])(halo(ds).start)
    each_peer(lambda k: raw_copy(k).start())
    raw[t, HALO : HALO + TX] = vol_ref[0, :, columns(t)]

    row = lax.broadcasted_iota(I32, (TX, PL), 0)
    col = lax.broadcasted_iota(I32, (TX, PL), 1)
    which = (col & 15) >> 3
    margin = jnp.where(col < 48, -EDGE, TX) + (col & 7)
    source = [
        jnp.where(col < TX, col, jnp.where(which == half, margin, 2 * PL)) for half in range(2)
    ]
    a = lax.broadcasted_iota(I32, (COLS, COLS), 0)
    b = lax.broadcasted_iota(I32, (COLS, COLS), 1)
    for i in range(2):
        for half in range(2):
            across[i, half] = band(shift_ref[i, 0, 0, 0], row - source[half]).astype(BF16)
        third = band(shift_ref[i, 0, 0, 2], (b & 63) - (a & 63))
        for d in range(4):
            second = band(shift_ref[i, 0, 0, 1], (b >> 6) - (a >> 6) - 4 * (d - 2))
            planes[i, d] = (second * third).astype(BF16)
    xw[0:64] = jnp.zeros((64, COLS), BF16)
    xw[18 * TX : 19 * TX] = jnp.zeros((TX, COLS), BF16)
    for k, ds, at in ((0, -1, 0), (1, 1, 48)):

        @pl.when(jnp.logical_not(there[ds]))
        def _():
            edge[k] = jnp.zeros((HALO, HALF), BF16)
            raw[:, at : at + HALO] = jnp.zeros((NT, HALO, COLS), BF16)
            win[:, :, at : at + HALO] = jnp.zeros((2, 3, HALO, COLS), BF16)
    for ds in (-1, 1):
        pl.when(from_side[ds])(halo(ds).wait_recv)

    def warp(i):
        for c in range(NT):
            half, at = c // 8, (c % 8) * COLS
            rows = [vol_ref[0, :, c * COLS : (c + 1) * COLS]]
            rows += [edge[k, :, at : at + COLS] for k in range(2)]
            xw[(c + 2) * TX : (c + 3) * TX] = jnp.dot(
                across[i, half], jnp.concatenate(rows, axis=0), preferred_element_type=F32
            ).astype(BF16)
        total = jnp.dot(xw[0 : NT * TX], planes[i, 0], preferred_element_type=F32)
        for d in range(1, 4):
            total += jnp.dot(
                xw[d * TX : (d + NT) * TX], planes[i, d], preferred_element_type=F32
            )
        return total.astype(BF16)

    cur[...] = warp(0).reshape(NT, TX, COLS)

    def cur_copy(k):
        to = lax.rem(x + k, 4)
        return remote(
            cur.at[pl.ds(4 * to, 4)], got.at[x], cur_send.at[k], cur_recv.at[k],
            (4 * to + z, s),
        )

    for k in (2, 1, 3):
        cur_copy(k).start()
    got[x] = cur[pl.ds(4 * x, 4)]
    for k in (1, 3, 2):
        cur_copy(k).wait_recv()
    sums[...] = jnp.sum(got[...].astype(F32), axis=0).astype(BF16)

    def share_copy(k):
        to = 4 * x + lax.rem(z + k, 4)
        return remote(
            sums.at[snake(to) - 4 * x], shares.at[z], share_send.at[k], share_recv.at[k], (to, s)
        )

    for k in (2, 1, 3):
        share_copy(k).start()
    shares[z] = sums[chunk - 4 * x]

    def win_copy(i, side, act):
        dt, ds = SIDES[side]
        src = {0: HALO, -1: HALO, 1: TX}[ds]
        dst = {0: HALO, -1: 48, 1: 0}[ds]
        rows = TX if ds == 0 else HALO
        copy = remote(
            win.at[i, 1, pl.ds(src, rows)], win.at[i, 1 - dt, pl.ds(dst, rows)],
            win_send.at[i, side], win_recv.at[i, side], (beside(dt), s + ds),
        )
        present = (from_side if act == "wait_recv" else there).get(ds)
        if present is None:
            getattr(copy, act)()
        else:
            pl.when(present)(getattr(copy, act))

    def windows(i, mean):
        win[i, 1, HALO : HALO + TX] = mean.astype(BF16)
        for side in range(8):
            win_copy(i, side, "start")

    each_peer(lambda k: raw_copy(k).wait_recv())
    windows(0, jnp.sum(raw[:, HALO : HALO + TX].astype(F32), axis=0) * (1.0 / NT))

    def rim(ds):
        src, dst = (HALO, 48) if ds < 0 else (TX, 0)
        k = 0 if ds < 0 else 1
        return remote(
            raw.at[:, pl.ds(src, HALO)], raw.at[:, pl.ds(dst, HALO)],
            rim_send.at[k], rim_recv.at[k], (t, s + ds),
        )

    for ds in (-1, 1):
        pl.when(there[ds])(rim(ds).start)

    second_warp = warp(1)
    for c in range(NT):
        reg_ref[0, :, c * COLS : (c + 1) * COLS] = second_warp[c * TX : (c + 1) * TX]

    for k in (1, 3, 2):
        share_copy(k).wait_recv()
    mean = jnp.sum(shares[...].astype(F32), axis=0) * (1.0 / NT)
    windows(1, mean)
    to_place = remote(
        mean_out, tmpl_ref, mean_send, mean_recv, (chunk, s)
    )

    mean_out[...] = mean
    put_mean = pltpu.make_async_copy(mean_out, tmpl_ref, local_sem)
    pl.when(chunk == t)(put_mean.start)
    pl.when(chunk != t)(to_place.start)

    for ds in (-1, 1):
        pl.when(from_side[ds])(rim(ds).wait_recv)
    for j in range(8):
        rows16 = raw[:, 16 * (j // 2) : 16 * (j // 2) + 16].astype(F32)
        eight = rows16[:, 8 * (j % 2) : 8 * (j % 2) + 8].reshape(NT * 8, COLS)
        turned[j] = eight.T.astype(BF16)

    lane = lax.broadcasted_iota(I32, (PL, 128), 1)
    place = lane & 63
    low_half = lane < 64
    step_of = lax.broadcasted_iota(I32, (128, 128), 1) & 7
    owner = lax.broadcasted_iota(I32, (NT, 128), 1) >> 3
    pick = (owner == lax.broadcasted_iota(I32, (NT, 128), 0)).astype(BF16)

    def correlate(i):
        blocks = []
        for half in range(6):
            x = win[i, half // 2, :, 128 * (half % 2) : 128 * (half % 2) + 128].astype(F32)
            blocks.append(pltpu.roll(x, 3, 0))

        def both(x):
            return jnp.concatenate([x, x[8:], x[:8]], axis=0).astype(BF16)

        for j3 in range(8):
            lag = j3 - 4
            turn = [pltpu.roll(x, lag % 128, 1) if lag else x for x in blocks]
            other = [pltpu.roll(x, (lag + 64) % 128, 1) for x in blocks]
            if lag > 0:
                inside = place >= lag
            else:
                inside = place < PL + lag
            even = [jnp.where(inside, p, q) for p, q in zip(turn, other)]
            swapped = [jnp.where(inside, q, p) for p, q in zip(turn, other)]
            odd = [
                both(jnp.where(low_half, swapped[h], swapped[h + 1])) for h in range(5)
            ]
            even = [x if h == 0 else both(x) for h, x in enumerate(even)]
            total = jnp.zeros((128, 128), F32)
            for j in range(8):
                rows = slice((j % 2) * PL + 16 * (j // 2), (j % 2) * PL + 16 * (j // 2) + 16)
                stack = []
                for j2 in range(8):
                    off = 8 - j2
                    which = odd if off % 2 else even
                    h = off // 2
                    stack.append(jnp.concatenate([which[h][rows], which[h + 1][rows]], axis=1))
                total += jnp.dot(
                    jnp.concatenate(stack, axis=0), turned[j], preferred_element_type=F32
                )
            for bit in (1, 2, 4):
                total = jnp.where((step_of & bit) != 0, pltpu.roll(total, 128 - bit, 0), total)
            lagged[j3 * 64 : (j3 + 1) * 64] = total.reshape(8, 16, 128)[:, 0:8].reshape(64, 128)
        ordered = jnp.concatenate(
            [
                lagged[pl.ds(j2 * 8 + 7 - j1, 8, stride=64), :]
                for j1 in range(8)
                for j2 in range(8)
            ],
            axis=0,
        )
        upper = ordered.astype(BF16)
        lower = (ordered - upper.astype(F32)).astype(BF16)
        sums = sum(
            lax.dot_general(
                pick, x, (((1,), (1,)), ((), ())), preferred_element_type=F32
            )
            for x in (upper, lower)
        ) * (1.0 / float(PL) ** 3)
        for k in range(4):
            part[:, 4 * i + k, :] = sums[:, 128 * k : 128 * k + 128]

    for i in range(2):
        for side in range(8):
            win_copy(i, side, "wait_recv")
        correlate(i)

    def part_copy(k):
        to = peer(k)
        return remote(part.at[to], gath.at[t], part_send.at[k], part_recv.at[k], (to, s))

    each_peer(lambda k: part_copy(k).start())
    gath[t] = part[t]
    for ds in (-1, 1):
        pl.when(there[ds])(halo(ds).wait_send)
        pl.when(there[ds])(rim(ds).wait_send)
    each_peer(lambda k: raw_copy(k).wait_send())
    for k in range(1, 4):
        cur_copy(k).wait_send()
        share_copy(k).wait_send()
    for i in range(2):
        for side in range(8):
            win_copy(i, side, "wait_send")
    each_peer(lambda k: part_copy(k).wait_recv())
    final = jnp.sum(gath[...], axis=0)
    for i in range(2):
        for k in range(4):
            corr_ref[i, 0, :, 128 * k : 128 * k + 128] = final[4 * i + k : 4 * i + k + 1]
    each_peer(lambda k: part_copy(k).wait_send())
    pl.when(chunk == t)(put_mean.wait)
    pl.when(chunk != t)(to_place.wait)


def put(*refs):
    *arrays, sems = refs
    copies = [pltpu.make_async_copy(arrays[k], arrays[k + 3], sems.at[k]) for k in range(3)]
    for copy in copies:
        copy.start()
    for copy in copies:
        copy.wait()


def solution(mesh):
    ns = mesh.shape["space"]

    def on_device(volumes, shifts):
        dma = pltpu.SemaphoreType.DMA
        vmem = pltpu.VMEM
        results = pl.pallas_call(
            functools.partial(kernel, ns),
            out_shape=(
                jax.ShapeDtypeStruct((2, 1, 1, 512), F32),
                jax.ShapeDtypeStruct((1, TX, PL * PL), BF16),
                jax.ShapeDtypeStruct((TX, COLS), F32),
            ),
            in_specs=[
                pl.BlockSpec(memory_space=pltpu.VMEM),
                pl.BlockSpec(memory_space=pltpu.SMEM),
            ],
            out_specs=(
                pl.BlockSpec(memory_space=pltpu.VMEM),
                pl.BlockSpec(memory_space=pltpu.VMEM),
                pl.BlockSpec(memory_space=pltpu.VMEM),
            ),
            scratch_shapes=[
                vmem((2, HALO, HALF), BF16),
                vmem((2, HALO, HALF), BF16),
                vmem((NT, PL, COLS), BF16),
                vmem((2, 2, TX, PL), BF16),
                vmem((2, 4, COLS, COLS), BF16),
                vmem(((NT + 3) * TX, COLS), BF16),
                vmem((NT, TX, COLS), BF16),
                vmem((4, 4, TX, COLS), BF16),
                vmem((4, TX, COLS), BF16),
                vmem((4, TX, COLS), BF16),
                vmem((2, 3, PL, COLS), BF16),
                vmem((8, COLS, 128), BF16),
                vmem((TX, COLS), F32),
                vmem((512, 128), F32),
                vmem((NT, 8, 128), F32),
                vmem((NT, 8, 128), F32),
                dma,
                dma((2,)), dma((2,)),
                dma((NT,)), dma((NT,)),
                dma((2,)), dma((2,)),
                dma((4,)), dma((4,)),
                dma((4,)), dma((4,)),
                dma((2, 8)), dma((2, 8)),
                dma, dma,
                dma((NT,)), dma((NT,)),
            ],
            compiler_params=pltpu.CompilerParams(
                collective_id=0, has_side_effects=True, vmem_limit_bytes=40 * 1024 * 1024
            ),
        )(volumes, shifts.transpose(0, 2, 3, 1))
        return pl.pallas_call(
            put,
            out_shape=tuple(jax.ShapeDtypeStruct(x.shape, x.dtype) for x in results),
            in_specs=[pl.BlockSpec(memory_space=pl.ANY)] * 3,
            out_specs=(pl.BlockSpec(memory_space=pl.ANY),) * 3,
            scratch_shapes=[dma((3,))],
            compiler_params=pltpu.CompilerParams(vmem_limit_bytes=1024 * 1024),
        )(*results)

    return jax.shard_map(
        on_device,
        mesh=mesh,
        in_specs=(P("tm", "space", None), P(None, None, "tm", "space")),
        out_specs=(P(None, "tm", "space", None), P("tm", "space", None), P("space", "tm")),
        check_vma=False,
    )
```

```python
import functools

import jax
import jax.numpy as jnp
from jax import lax
from jax.experimental import pallas as pl
from jax.experimental.pallas import tpu as pltpu
from jax.sharding import PartitionSpec as P

MESH = pl.DeviceIdType.MESH
F32, BF16, I32 = jnp.float32, jnp.bfloat16, jnp.int32

PL = 64
TX = 32
HALO = 16
NT = 16
COLS = 256
EDGE = 8
HALF = PL * PL // 2
OFFSETS = (
    (2, 2), (2, 1), (2, 3), (1, 2), (3, 2), (1, 1), (1, 3), (3, 1), (3, 3),
    (0, 2), (0, 1), (0, 3), (2, 0), (1, 0), (3, 0),
)
SIDES = tuple((dt, ds) for ds in (-1, 1, 0) for dt in (-1, 0, 1) if (dt, ds) != (0, 0))


def band(shift, delta):
    whole = jnp.right_shift(shift, 2)
    fraction = (shift - 4 * whole).astype(F32) * 0.25
    return jnp.where(
        delta == whole, 1.0 - fraction, jnp.where(delta == whole + 1, fraction, 0.0)
    )


def snake(t):
    z = lax.rem(t, 4)
    return t + lax.rem(t // 4, 2) * (3 - 2 * z)


def kernel(
    ns, vol_ref, shift_ref, corr_ref, reg_ref, tmpl_ref,
    edge_out, edge, raw, across, planes, xw, cur, got, sums, shares, rest, rests, win, turned, mean_out,
    lagged, part, gath,
    local_sem, halo_send, halo_recv, raw_send, raw_recv, rim_send, rim_recv,
    cur_send, cur_recv, share_send, share_recv, rest_send, rest_recv, win_send, win_recv, mean_send, mean_recv, part_send, part_recv,
):
    t = lax.axis_index("tm")
    s = lax.axis_index("space")
    chunk = snake(t)
    has_lo, has_hi = s > 0, s < ns - 1
    there = {-1: has_lo, 1: has_hi}
    from_side = {-1: has_hi, 1: has_lo}

    def peer(k):
        dx, dz = OFFSETS[k]
        return 4 * lax.rem(t // 4 + dx, 4) + lax.rem(lax.rem(t, 4) + dz, 4)

    def beside(dt):
        return snake(lax.rem(chunk + dt + NT, NT))

    x, z = t // 4, lax.rem(t, 4)

    def columns(to):
        return pl.ds(pl.multiple_of(snake(to) * COLS, COLS), COLS)

    def each_peer(body):
        for k in range(NT - 1):
            body(k)

    def remote(src, dst, send, recv, peer):
        return pltpu.make_async_remote_copy(
            src_ref=src, dst_ref=dst, send_sem=send, recv_sem=recv,
            device_id=peer, device_id_type=MESH,
        )

    barrier = pltpu.get_barrier_semaphore()
    each_peer(
        lambda k: pl.semaphore_signal(
            barrier, inc=1, device_id=(peer(k), s), device_id_type=MESH
        )
    )
    for ds in (-1, 1):

        @pl.when(there[ds])
        def _():
            for dt in (-1, 0, 1):
                pl.semaphore_signal(
                    barrier, inc=1, device_id=(beside(dt), s + ds), device_id_type=MESH
                )

    def source_of(col, half):
        margin = jnp.where(col < 48, -EDGE, TX) + (col & 7)
        return jnp.where(col < TX, col, jnp.where((col & 15) >> 3 == half, margin, 2 * PL))

    a = lax.broadcasted_iota(I32, (COLS, COLS), 0)
    b = lax.broadcasted_iota(I32, (COLS, COLS), 1)

    def plane_tables(i):
        third = band(shift_ref[i, 0, 0, 2], (b & 63) - (a & 63))
        for d in range(4):
            second = band(shift_ref[i, 0, 0, 1], (b >> 6) - (a >> 6) - 4 * (d - 2))
            planes[i, d] = (second * third).astype(BF16)

    def in_planes(i, n):
        total = jnp.dot(xw[0 : NT * n], planes[i, 0], preferred_element_type=F32)
        for d in range(1, 4):
            total += jnp.dot(
                xw[d * n : (d + NT) * n], planes[i, d], preferred_element_type=F32
            )
        return total.astype(BF16)

    plane_tables(0)
    row = lax.broadcasted_iota(I32, (TX, TX), 0)
    col = lax.broadcasted_iota(I32, (TX, TX), 1)
    from_own = band(shift_ref[0, 0, 0, 0], row - col).astype(BF16)
    xw[0:64] = jnp.zeros((64, COLS), BF16)
    xw[18 * TX : 19 * TX] = jnp.zeros((TX, COLS), BF16)
    for c in range(NT):
        xw[(c + 2) * TX : (c + 3) * TX] = jnp.dot(
            from_own, vol_ref[0, :, c * COLS : (c + 1) * COLS], preferred_element_type=F32
        ).astype(BF16)
    cur[...] = in_planes(0, TX).reshape(NT, TX, COLS)

    for k in range(2):
        wide = vol_ref[0, HALO * k : HALO * k + HALO].astype(F32)[EDGE * k : EDGE * k + EDGE]
        edge_out[k] = jnp.concatenate([wide[:, :HALF], wide[:, HALF:]], axis=0).astype(BF16)
    pl.semaphore_wait(barrier, NT - 1 + 3 * (has_lo.astype(I32) + has_hi.astype(I32)))

    def halo(ds):
        k = 0 if ds < 0 else 1
        return remote(
            edge_out.at[k], edge.at[1 - k], halo_send.at[k], halo_recv.at[k], (t, s + ds)
        )

    def raw_copy(k):
        to = peer(k)
        return remote(
            vol_ref.at[0, :, columns(to)], raw.at[t, pl.ds(HALO, TX)],
            raw_send.at[k], raw_recv.at[k], (to, s),
        )

    def cur_copy(k):
        to = lax.rem(x + k, 4)
        return remote(
            cur.at[pl.ds(4 * to, 4)], got.at[x], cur_send.at[k], cur_recv.at[k],
            (4 * to + z, s),
        )

    for ds in (-1, 1):
        pl.when(there[ds])(halo(ds).start)
    for k in (2, 1, 3):
        cur_copy(k).start()
    each_peer(lambda k: raw_copy(k).start())
    got[x] = cur[pl.ds(4 * x, 4)]
    raw[t, HALO : HALO + TX] = vol_ref[0, :, columns(t)]

    for k, ds, at in ((0, -1, 0), (1, 1, 48)):

        @pl.when(jnp.logical_not(there[ds]))
        def _():
            edge[k] = jnp.zeros((HALO, HALF), BF16)
            raw[:, at : at + HALO] = jnp.zeros((NT, HALO, COLS), BF16)
            win[:, :, at : at + HALO] = jnp.zeros((2, 3, HALO, COLS), BF16)

    row = lax.broadcasted_iota(I32, (TX, PL), 0)
    col = lax.broadcasted_iota(I32, (TX, PL), 1)
    for half in range(2):
        across[half] = band(shift_ref[1, 0, 0, 0], row - source_of(col, half)).astype(BF16)
    row = lax.broadcasted_iota(I32, (HALO, TX), 0)
    row = jnp.where(row < EDGE, row, row + HALO)
    col = lax.broadcasted_iota(I32, (HALO, TX), 1) + TX
    from_margins = [
        band(shift_ref[0, 0, 0, 0], row - source_of(col, half)).astype(BF16) for half in range(2)
    ]
    plane_tables(1)
    for ds in (-1, 1):
        pl.when(from_side[ds])(halo(ds).wait_recv)

    for c in range(NT):
        half, at = c // 8, (c % 8) * COLS
        rows = jnp.concatenate([edge[k, :, at : at + COLS] for k in range(2)], axis=0)
        xw[(c + 2) * HALO : (c + 3) * HALO] = jnp.dot(
            from_margins[half], rows, preferred_element_type=F32
        ).astype(BF16)
    xw[18 * HALO : 19 * HALO] = jnp.zeros((HALO, COLS), BF16)
    rest[...] = in_planes(0, HALO).reshape(NT, HALO, COLS)

    def rest_copy(k):
        to = peer(k)
        return remote(rest.at[snake(to)], rests.at[t], rest_send.at[k], rest_recv.at[k], (to, s))

    each_peer(lambda k: rest_copy(k).start())
    rests[t] = rest[chunk]

    for k in (1, 3, 2):
        cur_copy(k).wait_recv()
    sums[...] = jnp.sum(got[...].astype(F32), axis=0).astype(BF16)

    def share_copy(k):
        to = 4 * x + lax.rem(z + k, 4)
        return remote(
            sums.at[snake(to) - 4 * x], shares.at[z], share_send.at[k], share_recv.at[k], (to, s)
        )

    for k in (2, 1, 3):
        share_copy(k).start()
    shares[z] = sums[chunk - 4 * x]

    def win_copy(i, side, act):
        dt, ds = SIDES[side]
        src = {0: HALO, -1: HALO, 1: TX}[ds]
        dst = {0: HALO, -1: 48, 1: 0}[ds]
        rows = TX if ds == 0 else HALO
        copy = remote(
            win.at[i, 1, pl.ds(src, rows)], win.at[i, 1 - dt, pl.ds(dst, rows)],
            win_send.at[i, side], win_recv.at[i, side], (beside(dt), s + ds),
        )
        present = (from_side if act == "wait_recv" else there).get(ds)
        if present is None:
            getattr(copy, act)()
        else:
            pl.when(present)(getattr(copy, act))

    def windows(i, mean):
        win[i, 1, HALO : HALO + TX] = mean.astype(BF16)
        for side in range(8):
            win_copy(i, side, "start")

    each_peer(lambda k: raw_copy(k).wait_recv())
    windows(0, jnp.sum(raw[:, HALO : HALO + TX].astype(F32), axis=0) * (1.0 / NT))

    def rim(ds):
        src, dst = (HALO, 48) if ds < 0 else (TX, 0)
        k = 0 if ds < 0 else 1
        return remote(
            raw.at[:, pl.ds(src, HALO)], raw.at[:, pl.ds(dst, HALO)],
            rim_send.at[k], rim_recv.at[k], (t, s + ds),
        )

    for ds in (-1, 1):
        pl.when(there[ds])(rim(ds).start)

    xw[0:64] = jnp.zeros((64, COLS), BF16)
    xw[18 * TX : 19 * TX] = jnp.zeros((TX, COLS), BF16)
    for c in range(NT):
        half, at = c // 8, (c % 8) * COLS
        rows = [vol_ref[0, :, c * COLS : (c + 1) * COLS]]
        rows += [edge[k, :, at : at + COLS] for k in range(2)]
        xw[(c + 2) * TX : (c + 3) * TX] = jnp.dot(
            across[half], jnp.concatenate(rows, axis=0), preferred_element_type=F32
        ).astype(BF16)
    second_warp = in_planes(1, TX)
    for c in range(NT):
        reg_ref[0, :, c * COLS : (c + 1) * COLS] = second_warp[c * TX : (c + 1) * TX]

    for k in (1, 3, 2):
        share_copy(k).wait_recv()
    each_peer(lambda k: rest_copy(k).wait_recv())
    mean = jnp.sum(shares[...].astype(F32), axis=0)
    added = jnp.sum(rests[...].astype(F32), axis=0)
    mean = jnp.concatenate(
        [mean[0:8] + added[0:8], mean[8:24], mean[24:32] + added[8:16]], axis=0
    ) * (1.0 / NT)
    windows(1, mean)
    to_place = remote(
        mean_out, tmpl_ref, mean_send, mean_recv, (chunk, s)
    )

    mean_out[...] = mean
    put_mean = pltpu.make_async_copy(mean_out, tmpl_ref, local_sem)
    pl.when(chunk == t)(put_mean.start)
    pl.when(chunk != t)(to_place.start)

    for ds in (-1, 1):
        pl.when(from_side[ds])(rim(ds).wait_recv)
    for j in range(8):
        rows16 = raw[:, 16 * (j // 2) : 16 * (j // 2) + 16].astype(F32)
        eight = rows16[:, 8 * (j % 2) : 8 * (j % 2) + 8].reshape(NT * 8, COLS)
        turned[j] = eight.T.astype(BF16)

    lane = lax.broadcasted_iota(I32, (PL, 128), 1)
    place = lane & 63
    low_half = lane < 64
    step_of = lax.broadcasted_iota(I32, (128, 128), 1) & 7
    owner = lax.broadcasted_iota(I32, (NT, 128), 1) >> 3
    pick = (owner == lax.broadcasted_iota(I32, (NT, 128), 0)).astype(BF16)

    def correlate(i):
        blocks = []
        for half in range(6):
            x = win[i, half // 2, :, 128 * (half % 2) : 128 * (half % 2) + 128].astype(F32)
            blocks.append(pltpu.roll(x, 3, 0))

        def both(x):
            return jnp.concatenate([x, x[8:], x[:8]], axis=0).astype(BF16)

        for j3 in range(8):
            lag = j3 - 4
            turn = [pltpu.roll(x, lag % 128, 1) if lag else x for x in blocks]
            other = [pltpu.roll(x, (lag + 64) % 128, 1) for x in blocks]
            if lag > 0:
                inside = place >= lag
            else:
                inside = place < PL + lag
            even = [jnp.where(inside, p, q) for p, q in zip(turn, other)]
            swapped = [jnp.where(inside, q, p) for p, q in zip(turn, other)]
            odd = [
                both(jnp.where(low_half, swapped[h], swapped[h + 1])) for h in range(5)
            ]
            even = [x if h == 0 else both(x) for h, x in enumerate(even)]
            total = jnp.zeros((128, 128), F32)
            for j in range(8):
                rows = slice((j % 2) * PL + 16 * (j // 2), (j % 2) * PL + 16 * (j // 2) + 16)
                stack = []
                for j2 in range(8):
                    off = 8 - j2
                    which = odd if off % 2 else even
                    h = off // 2
                    stack.append(jnp.concatenate([which[h][rows], which[h + 1][rows]], axis=1))
                total += jnp.dot(
                    jnp.concatenate(stack, axis=0), turned[j], preferred_element_type=F32
                )
            for bit in (1, 2, 4):
                total = jnp.where((step_of & bit) != 0, pltpu.roll(total, 128 - bit, 0), total)
            lagged[j3 * 64 : (j3 + 1) * 64] = total.reshape(8, 16, 128)[:, 0:8].reshape(64, 128)
        ordered = jnp.concatenate(
            [
                lagged[pl.ds(j2 * 8 + 7 - j1, 8, stride=64), :]
                for j1 in range(8)
                for j2 in range(8)
            ],
            axis=0,
        )
        upper = ordered.astype(BF16)
        lower = (ordered - upper.astype(F32)).astype(BF16)
        sums = sum(
            lax.dot_general(
                pick, x, (((1,), (1,)), ((), ())), preferred_element_type=F32
            )
            for x in (upper, lower)
        ) * (1.0 / float(PL) ** 3)
        for k in range(4):
            part[:, 4 * i + k, :] = sums[:, 128 * k : 128 * k + 128]

    for i in range(2):
        for side in range(8):
            win_copy(i, side, "wait_recv")
        correlate(i)

    def part_copy(k):
        to = peer(k)
        return remote(part.at[to], gath.at[t], part_send.at[k], part_recv.at[k], (to, s))

    each_peer(lambda k: part_copy(k).start())
    gath[t] = part[t]
    for ds in (-1, 1):
        pl.when(there[ds])(halo(ds).wait_send)
        pl.when(there[ds])(rim(ds).wait_send)
    each_peer(lambda k: raw_copy(k).wait_send())
    for k in range(1, 4):
        cur_copy(k).wait_send()
        share_copy(k).wait_send()
    each_peer(lambda k: rest_copy(k).wait_send())
    for i in range(2):
        for side in range(8):
            win_copy(i, side, "wait_send")
    each_peer(lambda k: part_copy(k).wait_recv())
    final = jnp.sum(gath[...], axis=0)
    for i in range(2):
        for k in range(4):
            corr_ref[i, 0, :, 128 * k : 128 * k + 128] = final[4 * i + k : 4 * i + k + 1]
    each_peer(lambda k: part_copy(k).wait_send())
    pl.when(chunk == t)(put_mean.wait)
    pl.when(chunk != t)(to_place.wait)


def put(*refs):
    *arrays, sems = refs
    copies = [pltpu.make_async_copy(arrays[k], arrays[k + 3], sems.at[k]) for k in range(3)]
    for copy in copies:
        copy.start()
    for copy in copies:
        copy.wait()


def solution(mesh):
    ns = mesh.shape["space"]

    def on_device(volumes, shifts):
        dma = pltpu.SemaphoreType.DMA
        vmem = pltpu.VMEM
        results = pl.pallas_call(
            functools.partial(kernel, ns),
            out_shape=(
                jax.ShapeDtypeStruct((2, 1, 1, 512), F32),
                jax.ShapeDtypeStruct((1, TX, PL * PL), BF16),
                jax.ShapeDtypeStruct((TX, COLS), F32),
            ),
            in_specs=[
                pl.BlockSpec(memory_space=pltpu.VMEM),
                pl.BlockSpec(memory_space=pltpu.SMEM),
            ],
            out_specs=(
                pl.BlockSpec(memory_space=pltpu.VMEM),
                pl.BlockSpec(memory_space=pltpu.VMEM),
                pl.BlockSpec(memory_space=pltpu.VMEM),
            ),
            scratch_shapes=[
                vmem((2, HALO, HALF), BF16),
                vmem((2, HALO, HALF), BF16),
                vmem((NT, PL, COLS), BF16),
                vmem((2, TX, PL), BF16),
                vmem((2, 4, COLS, COLS), BF16),
                vmem(((NT + 3) * TX, COLS), BF16),
                vmem((NT, TX, COLS), BF16),
                vmem((4, 4, TX, COLS), BF16),
                vmem((4, TX, COLS), BF16),
                vmem((4, TX, COLS), BF16),
                vmem((NT, HALO, COLS), BF16),
                vmem((NT, HALO, COLS), BF16),
                vmem((2, 3, PL, COLS), BF16),
                vmem((8, COLS, 128), BF16),
                vmem((TX, COLS), F32),
                vmem((512, 128), F32),
                vmem((NT, 8, 128), F32),
                vmem((NT, 8, 128), F32),
                dma,
                dma((2,)), dma((2,)),
                dma((NT,)), dma((NT,)),
                dma((2,)), dma((2,)),
                dma((4,)), dma((4,)),
                dma((4,)), dma((4,)),
                dma((NT,)), dma((NT,)),
                dma((2, 8)), dma((2, 8)),
                dma, dma,
                dma((NT,)), dma((NT,)),
            ],
            compiler_params=pltpu.CompilerParams(
                collective_id=0, has_side_effects=True, vmem_limit_bytes=40 * 1024 * 1024
            ),
        )(volumes, shifts.transpose(0, 2, 3, 1))
        return pl.pallas_call(
            put,
            out_shape=tuple(jax.ShapeDtypeStruct(x.shape, x.dtype) for x in results),
            in_specs=[pl.BlockSpec(memory_space=pl.ANY)] * 3,
            out_specs=(pl.BlockSpec(memory_space=pl.ANY),) * 3,
            scratch_shapes=[dma((3,))],
            compiler_params=pltpu.CompilerParams(vmem_limit_bytes=1024 * 1024),
        )(*results)

    return jax.shard_map(
        on_device,
        mesh=mesh,
        in_specs=(P("tm", "space", None), P(None, None, "tm", "space")),
        out_specs=(P(None, "tm", "space", None), P("tm", "space", None), P("space", "tm")),
        check_vma=False,
    )
```

```python
import functools

import jax
import jax.numpy as jnp
from jax import lax
from jax.experimental import pallas as pl
from jax.experimental.pallas import tpu as pltpu
from jax.sharding import PartitionSpec as P

MESH = pl.DeviceIdType.MESH
F32, BF16, I32 = jnp.float32, jnp.bfloat16, jnp.int32

PL = 64
TX = 32
HALO = 16
NT = 16
COLS = 256
EDGE = 4
QUARTER = PL * PL // 4
OFFSETS = (
    (2, 2), (2, 1), (2, 3), (1, 2), (3, 2), (1, 1), (1, 3), (3, 1), (3, 3),
    (0, 2), (0, 1), (0, 3), (2, 0), (1, 0), (3, 0),
)
SIDES = tuple((dt, ds) for ds in (-1, 1, 0) for dt in (-1, 0, 1) if (dt, ds) != (0, 0))


def band(shift, delta):
    whole = jnp.right_shift(shift, 2)
    fraction = (shift - 4 * whole).astype(F32) * 0.25
    return jnp.where(
        delta == whole, 1.0 - fraction, jnp.where(delta == whole + 1, fraction, 0.0)
    )


def snake(t):
    z = lax.rem(t, 4)
    return t + lax.rem(t // 4, 2) * (3 - 2 * z)


def kernel(
    ns, vol_ref, shift_ref, corr_ref, reg_ref, tmpl_ref,
    edge_out, edge, raw, across, planes, xw, cur, got, sums, shares, rest, rests, win, turned, mean_out,
    lagged, part, gath,
    local_sem, halo_send, halo_recv, raw_send, raw_recv, rim_send, rim_recv,
    cur_send, cur_recv, share_send, share_recv, rest_send, rest_recv, far_send, far_recv, win_send, win_recv, mean_send, mean_recv, part_send, part_recv,
):
    t = lax.axis_index("tm")
    s = lax.axis_index("space")
    chunk = snake(t)
    has_lo, has_hi = s > 0, s < ns - 1
    there = {-1: has_lo, 1: has_hi}
    from_side = {-1: has_hi, 1: has_lo}
    below, above = s == ns // 2 - 1, s == ns // 2
    far = {-1: above, 1: below}
    from_far = {-1: below, 1: above}

    def peer(k):
        dx, dz = OFFSETS[k]
        return 4 * lax.rem(t // 4 + dx, 4) + lax.rem(lax.rem(t, 4) + dz, 4)

    def beside(dt):
        return snake(lax.rem(chunk + dt + NT, NT))

    x, z = t // 4, lax.rem(t, 4)

    def columns(to):
        return pl.ds(pl.multiple_of(snake(to) * COLS, COLS), COLS)

    def each_peer(body):
        for k in range(NT - 1):
            body(k)

    def remote(src, dst, send, recv, peer):
        return pltpu.make_async_remote_copy(
            src_ref=src, dst_ref=dst, send_sem=send, recv_sem=recv,
            device_id=peer, device_id_type=MESH,
        )

    barrier = pltpu.get_barrier_semaphore()
    each_peer(
        lambda k: pl.semaphore_signal(
            barrier, inc=1, device_id=(peer(k), s), device_id_type=MESH
        )
    )
    for ds in (-1, 1):

        @pl.when(there[ds])
        def _():
            for dt in (-1, 0, 1):
                pl.semaphore_signal(
                    barrier, inc=1, device_id=(beside(dt), s + ds), device_id_type=MESH
                )

    for ds in (-1, 1):

        @pl.when(far[ds])
        def _():
            for k in range(NT - 1):
                pl.semaphore_signal(
                    barrier, inc=1, device_id=(peer(k), s + ds), device_id_type=MESH
                )

    def source_of(col, part):
        margin = jnp.where(col < 48, -EDGE, TX) + (col & 3)
        return jnp.where(col < TX, col, jnp.where((col & 15) >> 2 == part, margin, 2 * PL))

    a = lax.broadcasted_iota(I32, (COLS, COLS), 0)
    b = lax.broadcasted_iota(I32, (COLS, COLS), 1)

    def plane_tables(i):
        third = band(shift_ref[i, 0, 0, 2], (b & 63) - (a & 63))
        for d in range(4):
            second = band(shift_ref[i, 0, 0, 1], (b >> 6) - (a >> 6) - 4 * (d - 2))
            planes[i, d] = (second * third).astype(BF16)

    def in_planes(i, n, dtype=BF16):
        total = jnp.dot(xw[0 : NT * n], planes[i, 0], preferred_element_type=F32)
        for d in range(1, 4):
            total += jnp.dot(
                xw[d * n : (d + NT) * n], planes[i, d], preferred_element_type=F32
            )
        return total.astype(dtype)

    plane_tables(0)
    row = lax.broadcasted_iota(I32, (TX, TX), 0)
    col = lax.broadcasted_iota(I32, (TX, TX), 1)
    from_own = band(shift_ref[0, 0, 0, 0], row - col).astype(BF16)
    xw[0:64] = jnp.zeros((64, COLS), BF16)
    xw[18 * TX : 19 * TX] = jnp.zeros((TX, COLS), BF16)
    for c in range(NT):
        xw[(c + 2) * TX : (c + 3) * TX] = jnp.dot(
            from_own, vol_ref[0, :, c * COLS : (c + 1) * COLS], preferred_element_type=F32
        ).astype(BF16)
    cur[...] = in_planes(0, TX).reshape(NT, TX, COLS)

    for k in range(2):
        wide = vol_ref[0, HALO * k : HALO * k + HALO].astype(F32)[12 * k : 12 * k + EDGE]
        edge_out[k] = jnp.concatenate(
            [wide[:, QUARTER * q : QUARTER * q + QUARTER] for q in range(4)], axis=0
        ).astype(BF16)
    pl.semaphore_wait(
        barrier,
        NT - 1
        + 3 * (has_lo.astype(I32) + has_hi.astype(I32))
        + (NT - 1) * (below.astype(I32) + above.astype(I32)),
    )

    def halo(ds):
        k = 0 if ds < 0 else 1
        return remote(
            edge_out.at[k], edge.at[1 - k], halo_send.at[k], halo_recv.at[k], (t, s + ds)
        )

    def raw_copy(k):
        to = peer(k)
        return remote(
            vol_ref.at[0, :, columns(to)], raw.at[t, pl.ds(HALO, TX)],
            raw_send.at[k], raw_recv.at[k], (to, s),
        )

    def cur_copy(k):
        to = lax.rem(x + k, 4)
        return remote(
            cur.at[pl.ds(4 * to, 4)], got.at[x], cur_send.at[k], cur_recv.at[k],
            (4 * to + z, s),
        )

    for ds in (-1, 1):
        pl.when(there[ds])(halo(ds).start)
    for k in (2, 1, 3):
        cur_copy(k).start()
    each_peer(lambda k: raw_copy(k).start())

    def far_copy(k, ds):
        to = t if k == NT - 1 else peer(k)
        src, dst = (0, 48) if ds < 0 else (HALO, 0)
        return remote(
            vol_ref.at[0, pl.ds(src, HALO), columns(to)], raw.at[t, pl.ds(dst, HALO)],
            far_send.at[k], far_recv.at[k], (to, s + ds),
        )

    def each_far(act, where):
        for ds in (-1, 1):

            @pl.when(where[ds])
            def _():
                for k in range(NT):
                    getattr(far_copy(k, ds), act)()

    each_far("start", far)
    got[x] = cur[pl.ds(4 * x, 4)]
    raw[t, HALO : HALO + TX] = vol_ref[0, :, columns(t)]

    for k, ds, at in ((0, -1, 0), (1, 1, 48)):

        @pl.when(jnp.logical_not(there[ds]))
        def _():
            edge[k] = jnp.zeros((HALO, QUARTER), BF16)
            raw[:, at : at + HALO] = jnp.zeros((NT, HALO, COLS), BF16)
            win[:, :, at : at + HALO] = jnp.zeros((2, 3, HALO, COLS), BF16)

    row = lax.broadcasted_iota(I32, (TX, PL), 0)
    col = lax.broadcasted_iota(I32, (TX, PL), 1)
    for part_of in range(4):
        across[part_of] = band(
            shift_ref[1, 0, 0, 0], row - source_of(col, part_of)
        ).astype(BF16)
    row = lax.broadcasted_iota(I32, (HALO, TX), 0)
    row = jnp.where(row < EDGE, row, jnp.where(row < 8, row + 24, 8 * PL))
    col = lax.broadcasted_iota(I32, (HALO, TX), 1) + TX
    from_margins = [
        band(shift_ref[0, 0, 0, 0], row - source_of(col, part_of)).astype(BF16)
        for part_of in range(4)
    ]
    plane_tables(1)
    for ds in (-1, 1):
        pl.when(from_side[ds])(halo(ds).wait_recv)

    for c in range(NT):
        at = (c % 4) * COLS
        rows = jnp.concatenate([edge[k, :, at : at + COLS] for k in range(2)], axis=0)
        xw[(c + 2) * HALO : (c + 3) * HALO] = jnp.dot(
            from_margins[c // 4], rows, preferred_element_type=F32
        ).astype(BF16)
    xw[18 * HALO : 19 * HALO] = jnp.zeros((HALO, COLS), BF16)
    eight = in_planes(0, HALO, F32).reshape(NT, HALO, COLS)[:, 0:8]
    rest[...] = jnp.concatenate([eight[:, :, :128], eight[:, :, 128:]], axis=1).astype(BF16)

    def rest_copy(k):
        to = peer(k)
        return remote(rest.at[snake(to)], rests.at[t], rest_send.at[k], rest_recv.at[k], (to, s))

    each_peer(lambda k: rest_copy(k).start())
    rests[t] = rest[chunk]

    for k in (1, 3, 2):
        cur_copy(k).wait_recv()
    sums[...] = jnp.sum(got[...].astype(F32), axis=0).astype(BF16)

    def share_copy(k):
        to = 4 * x + lax.rem(z + k, 4)
        return remote(
            sums.at[snake(to) - 4 * x], shares.at[z], share_send.at[k], share_recv.at[k], (to, s)
        )

    for k in (2, 1, 3):
        share_copy(k).start()
    shares[z] = sums[chunk - 4 * x]

    def win_copy(i, side, act):
        dt, ds = SIDES[side]
        src = {0: HALO, -1: HALO, 1: TX}[ds]
        dst = {0: HALO, -1: 48, 1: 0}[ds]
        rows = TX if ds == 0 else HALO
        copy = remote(
            win.at[i, 1, pl.ds(src, rows)], win.at[i, 1 - dt, pl.ds(dst, rows)],
            win_send.at[i, side], win_recv.at[i, side], (beside(dt), s + ds),
        )
        present = (from_side if act == "wait_recv" else there).get(ds)
        if present is None:
            getattr(copy, act)()
        else:
            pl.when(present)(getattr(copy, act))

    def windows(i, mean):
        win[i, 1, HALO : HALO + TX] = mean.astype(BF16)
        for side in range(8):
            win_copy(i, side, "start")

    each_peer(lambda k: raw_copy(k).wait_recv())
    windows(0, jnp.sum(raw[:, HALO : HALO + TX].astype(F32), axis=0) * (1.0 / NT))

    def rim(ds):
        src, dst = (HALO, 48) if ds < 0 else (TX, 0)
        k = 0 if ds < 0 else 1
        return remote(
            raw.at[:, pl.ds(src, HALO)], raw.at[:, pl.ds(dst, HALO)],
            rim_send.at[k], rim_recv.at[k], (t, s + ds),
        )

    near = {ds: there[ds] & jnp.logical_not(far[ds]) for ds in (-1, 1)}
    from_near = {ds: from_side[ds] & jnp.logical_not(from_far[ds]) for ds in (-1, 1)}
    for ds in (-1, 1):
        pl.when(near[ds])(rim(ds).start)

    xw[0:64] = jnp.zeros((64, COLS), BF16)
    xw[18 * TX : 19 * TX] = jnp.zeros((TX, COLS), BF16)
    for c in range(NT):
        at = (c % 4) * COLS
        rows = [vol_ref[0, :, c * COLS : (c + 1) * COLS]]
        rows += [edge[k, :, at : at + COLS] for k in range(2)]
        xw[(c + 2) * TX : (c + 3) * TX] = jnp.dot(
            across[c // 4], jnp.concatenate(rows, axis=0), preferred_element_type=F32
        ).astype(BF16)
    second_warp = in_planes(1, TX)
    for c in range(NT):
        reg_ref[0, :, c * COLS : (c + 1) * COLS] = second_warp[c * TX : (c + 1) * TX]

    for k in (1, 3, 2):
        share_copy(k).wait_recv()
    each_peer(lambda k: rest_copy(k).wait_recv())
    mean = jnp.sum(shares[...].astype(F32), axis=0)
    added = jnp.sum(rests[...].astype(F32), axis=0)
    added = jnp.concatenate([added[0:8], added[8:16]], axis=1)
    first = lax.broadcasted_iota(I32, (8, COLS), 0) < EDGE
    mean = jnp.concatenate(
        [
            mean[0:8] + jnp.where(first, added, 0.0),
            mean[8:24],
            mean[24:32] + jnp.where(first, 0.0, added),
        ],
        axis=0,
    ) * (1.0 / NT)
    windows(1, mean)
    to_place = remote(
        mean_out, tmpl_ref, mean_send, mean_recv, (chunk, s)
    )

    mean_out[...] = mean
    put_mean = pltpu.make_async_copy(mean_out, tmpl_ref, local_sem)
    pl.when(chunk == t)(put_mean.start)
    pl.when(chunk != t)(to_place.start)

    for ds in (-1, 1):
        pl.when(from_near[ds])(rim(ds).wait_recv)
    each_far("wait_recv", from_far)
    for j in range(8):
        rows16 = raw[:, 16 * (j // 2) : 16 * (j // 2) + 16].astype(F32)
        eight = rows16[:, 8 * (j % 2) : 8 * (j % 2) + 8].reshape(NT * 8, COLS)
        turned[j] = eight.T.astype(BF16)

    lane = lax.broadcasted_iota(I32, (PL, 128), 1)
    place = lane & 63
    low_half = lane < 64
    step_of = lax.broadcasted_iota(I32, (128, 128), 1) & 7
    owner = lax.broadcasted_iota(I32, (NT, 128), 1) >> 3
    pick = (owner == lax.broadcasted_iota(I32, (NT, 128), 0)).astype(BF16)

    def correlate(i):
        blocks = []
        for half in range(6):
            x = win[i, half // 2, :, 128 * (half % 2) : 128 * (half % 2) + 128].astype(F32)
            blocks.append(pltpu.roll(x, 3, 0))

        def both(x):
            return jnp.concatenate([x, x[8:], x[:8]], axis=0).astype(BF16)

        for j3 in range(8):
            lag = j3 - 4
            turn = [pltpu.roll(x, lag % 128, 1) if lag else x for x in blocks]
            other = [pltpu.roll(x, (lag + 64) % 128, 1) for x in blocks]
            if lag > 0:
                inside = place >= lag
            else:
                inside = place < PL + lag
            even = [jnp.where(inside, p, q) for p, q in zip(turn, other)]
            swapped = [jnp.where(inside, q, p) for p, q in zip(turn, other)]
            odd = [
                both(jnp.where(low_half, swapped[h], swapped[h + 1])) for h in range(5)
            ]
            even = [x if h == 0 else both(x) for h, x in enumerate(even)]
            total = jnp.zeros((128, 128), F32)
            for j in range(8):
                rows = slice((j % 2) * PL + 16 * (j // 2), (j % 2) * PL + 16 * (j // 2) + 16)
                stack = []
                for j2 in range(8):
                    off = 8 - j2
                    which = odd if off % 2 else even
                    h = off // 2
                    stack.append(jnp.concatenate([which[h][rows], which[h + 1][rows]], axis=1))
                total += jnp.dot(
                    jnp.concatenate(stack, axis=0), turned[j], preferred_element_type=F32
                )
            for bit in (1, 2, 4):
                total = jnp.where((step_of & bit) != 0, pltpu.roll(total, 128 - bit, 0), total)
            lagged[j3 * 64 : (j3 + 1) * 64] = total.reshape(8, 16, 128)[:, 0:8].reshape(64, 128)
        ordered = jnp.concatenate(
            [
                lagged[pl.ds(j2 * 8 + 7 - j1, 8, stride=64), :]
                for j1 in range(8)
                for j2 in range(8)
            ],
            axis=0,
        )
        upper = ordered.astype(BF16)
        lower = (ordered - upper.astype(F32)).astype(BF16)
        sums = sum(
            lax.dot_general(
                pick, x, (((1,), (1,)), ((), ())), preferred_element_type=F32
            )
            for x in (upper, lower)
        ) * (1.0 / float(PL) ** 3)
        for k in range(4):
            part[:, 4 * i + k, :] = sums[:, 128 * k : 128 * k + 128]

    for i in range(2):
        for side in range(8):
            win_copy(i, side, "wait_recv")
        correlate(i)

    def part_copy(k):
        to = peer(k)
        return remote(part.at[to], gath.at[t], part_send.at[k], part_recv.at[k], (to, s))

    each_peer(lambda k: part_copy(k).start())
    gath[t] = part[t]
    for ds in (-1, 1):
        pl.when(there[ds])(halo(ds).wait_send)
        pl.when(near[ds])(rim(ds).wait_send)
    each_far("wait_send", far)
    each_peer(lambda k: raw_copy(k).wait_send())
    for k in range(1, 4):
        cur_copy(k).wait_send()
        share_copy(k).wait_send()
    each_peer(lambda k: rest_copy(k).wait_send())
    for i in range(2):
        for side in range(8):
            win_copy(i, side, "wait_send")
    each_peer(lambda k: part_copy(k).wait_recv())
    final = jnp.sum(gath[...], axis=0)
    for i in range(2):
        for k in range(4):
            corr_ref[i, 0, :, 128 * k : 128 * k + 128] = final[4 * i + k : 4 * i + k + 1]
    each_peer(lambda k: part_copy(k).wait_send())
    pl.when(chunk == t)(put_mean.wait)
    pl.when(chunk != t)(to_place.wait)


def put(*refs):
    *arrays, sems = refs
    copies = [pltpu.make_async_copy(arrays[k], arrays[k + 3], sems.at[k]) for k in range(3)]
    for copy in copies:
        copy.start()
    for copy in copies:
        copy.wait()


def solution(mesh):
    ns = mesh.shape["space"]

    def on_device(volumes, shifts):
        dma = pltpu.SemaphoreType.DMA
        vmem = pltpu.VMEM
        results = pl.pallas_call(
            functools.partial(kernel, ns),
            out_shape=(
                jax.ShapeDtypeStruct((2, 1, 1, 512), F32),
                jax.ShapeDtypeStruct((1, TX, PL * PL), BF16),
                jax.ShapeDtypeStruct((TX, COLS), F32),
            ),
            in_specs=[
                pl.BlockSpec(memory_space=pltpu.VMEM),
                pl.BlockSpec(memory_space=pltpu.SMEM),
            ],
            out_specs=(
                pl.BlockSpec(memory_space=pltpu.VMEM),
                pl.BlockSpec(memory_space=pltpu.VMEM),
                pl.BlockSpec(memory_space=pltpu.VMEM),
            ),
            scratch_shapes=[
                vmem((2, HALO, QUARTER), BF16),
                vmem((2, HALO, QUARTER), BF16),
                vmem((NT, PL, COLS), BF16),
                vmem((4, TX, PL), BF16),
                vmem((2, 4, COLS, COLS), BF16),
                vmem(((NT + 3) * TX, COLS), BF16),
                vmem((NT, TX, COLS), BF16),
                vmem((4, 4, TX, COLS), BF16),
                vmem((4, TX, COLS), BF16),
                vmem((4, TX, COLS), BF16),
                vmem((NT, HALO, 128), BF16),
                vmem((NT, HALO, 128), BF16),
                vmem((2, 3, PL, COLS), BF16),
                vmem((8, COLS, 128), BF16),
                vmem((TX, COLS), F32),
                vmem((512, 128), F32),
                vmem((NT, 8, 128), F32),
                vmem((NT, 8, 128), F32),
                dma,
                dma((2,)), dma((2,)),
                dma((NT,)), dma((NT,)),
                dma((2,)), dma((2,)),
                dma((4,)), dma((4,)),
                dma((4,)), dma((4,)),
                dma((NT,)), dma((NT,)),
                dma((NT,)), dma((NT,)),
                dma((2, 8)), dma((2, 8)),
                dma, dma,
                dma((NT,)), dma((NT,)),
            ],
            compiler_params=pltpu.CompilerParams(
                collective_id=0, has_side_effects=True, vmem_limit_bytes=40 * 1024 * 1024
            ),
        )(volumes, shifts.transpose(0, 2, 3, 1))
        return pl.pallas_call(
            put,
            out_shape=tuple(jax.ShapeDtypeStruct(x.shape, x.dtype) for x in results),
            in_specs=[pl.BlockSpec(memory_space=pl.ANY)] * 3,
            out_specs=(pl.BlockSpec(memory_space=pl.ANY),) * 3,
            scratch_shapes=[dma((3,))],
            compiler_params=pltpu.CompilerParams(vmem_limit_bytes=1024 * 1024),
        )(*results)

    return jax.shard_map(
        on_device,
        mesh=mesh,
        in_specs=(P("tm", "space", None), P(None, None, "tm", "space")),
        out_specs=(P(None, "tm", "space", None), P("tm", "space", None), P("space", "tm")),
        check_vma=False,
    )
```

```python
import functools

import jax
import jax.numpy as jnp
from jax import lax
from jax.experimental import pallas as pl
from jax.experimental.pallas import tpu as pltpu
from jax.sharding import PartitionSpec as P

MESH = pl.DeviceIdType.MESH
F32, BF16, I32 = jnp.float32, jnp.bfloat16, jnp.int32

PL = 64
TX = 32
HALO = 16
NT = 16
COLS = 256
EDGE = 4
QUARTER = PL * PL // 4
OFFSETS = (
    (2, 2), (2, 1), (2, 3), (1, 2), (3, 2), (1, 1), (1, 3), (3, 1), (3, 3),
    (0, 2), (0, 1), (0, 3), (2, 0), (1, 0), (3, 0),
)
SIDES = tuple((dt, ds) for ds in (-1, 1, 0) for dt in (-1, 0, 1) if (dt, ds) != (0, 0))


def band(shift, delta):
    whole = jnp.right_shift(shift, 2)
    fraction = (shift - 4 * whole).astype(F32) * 0.25
    return jnp.where(
        delta == whole, 1.0 - fraction, jnp.where(delta == whole + 1, fraction, 0.0)
    )


def snake(t):
    z = lax.rem(t, 4)
    return t + lax.rem(t // 4, 2) * (3 - 2 * z)


def kernel(
    ns, vol_ref, shift_ref, corr_ref, reg_ref, tmpl_ref,
    edge_out, edge, raw, across, planes, xw, cur, got, sums, shares, rest, rests, over, overs, extras, apart, move, moved, far_planes, win, turned, mean_out,
    lagged, part, gath,
    local_sem, halo_send, halo_recv, raw_send, raw_recv, rim_send, rim_recv,
    cur_send, cur_recv, share_send, share_recv, rest_send, rest_recv, far_send, far_recv, over_send, over_recv, extra_send, extra_recv, move_send, move_recv,
    win_send, win_recv, mean_send, mean_recv, part_send, part_recv,
):
    t = lax.axis_index("tm")
    s = lax.axis_index("space")
    chunk = snake(t)
    has_lo, has_hi = s > 0, s < ns - 1
    there = {-1: has_lo, 1: has_hi}
    from_side = {-1: has_hi, 1: has_lo}
    below, above = s == ns // 2 - 1, s == ns // 2
    far = {-1: above, 1: below}
    from_far = {-1: below, 1: above}

    def peer(k):
        dx, dz = OFFSETS[k]
        return 4 * lax.rem(t // 4 + dx, 4) + lax.rem(lax.rem(t, 4) + dz, 4)

    def beside(dt):
        return snake(lax.rem(chunk + dt + NT, NT))

    x, z = t // 4, lax.rem(t, 4)

    def columns(to):
        return pl.ds(pl.multiple_of(snake(to) * COLS, COLS), COLS)

    def each_peer(body):
        for k in range(NT - 1):
            body(k)

    def remote(src, dst, send, recv, peer):
        return pltpu.make_async_remote_copy(
            src_ref=src, dst_ref=dst, send_sem=send, recv_sem=recv,
            device_id=peer, device_id_type=MESH,
        )

    barrier = pltpu.get_barrier_semaphore()
    each_peer(
        lambda k: pl.semaphore_signal(
            barrier, inc=1, device_id=(peer(k), s), device_id_type=MESH
        )
    )
    for ds in (-1, 1):

        @pl.when(there[ds])
        def _():
            for dt in (-1, 0, 1):
                pl.semaphore_signal(
                    barrier, inc=1, device_id=(beside(dt), s + ds), device_id_type=MESH
                )

    for ds in (-1, 1):

        @pl.when(far[ds])
        def _():
            for k in range(NT - 1):
                pl.semaphore_signal(
                    barrier, inc=1, device_id=(peer(k), s + ds), device_id_type=MESH
                )

    def source_of(col, part):
        margin = jnp.where(col < 48, -EDGE, TX) + (col & 3)
        return jnp.where(col < TX, col, jnp.where((col & 15) >> 2 == part, margin, 2 * PL))

    a = lax.broadcasted_iota(I32, (COLS, COLS), 0)
    b = lax.broadcasted_iota(I32, (COLS, COLS), 1)

    def plane_tables(i):
        third = band(shift_ref[i, 0, 0, 2], (b & 63) - (a & 63))
        for d in range(4):
            second = band(shift_ref[i, 0, 0, 1], (b >> 6) - (a >> 6) - 4 * (d - 2))
            planes[i, d] = (second * third).astype(BF16)

    def in_planes(i, n, dtype=BF16):
        total = jnp.dot(xw[0 : NT * n], planes[i, 0], preferred_element_type=F32)
        for d in range(1, 4):
            total += jnp.dot(
                xw[d * n : (d + NT) * n], planes[i, d], preferred_element_type=F32
            )
        return total.astype(dtype)

    row = lax.broadcasted_iota(I32, (8, 128), 0)
    move[...] = jnp.where(
        row == 0, shift_ref[0, 0, 0, 0], jnp.where(row == 1, shift_ref[0, 0, 0, 1], shift_ref[0, 0, 0, 2])
    )
    plane_tables(0)
    row = lax.broadcasted_iota(I32, (TX, TX), 0)
    col = lax.broadcasted_iota(I32, (TX, TX), 1)
    from_own = band(shift_ref[0, 0, 0, 0], row - col).astype(BF16)
    xw[0:64] = jnp.zeros((64, COLS), BF16)
    xw[18 * TX : 19 * TX] = jnp.zeros((TX, COLS), BF16)
    for c in range(NT):
        xw[(c + 2) * TX : (c + 3) * TX] = jnp.dot(
            from_own, vol_ref[0, :, c * COLS : (c + 1) * COLS], preferred_element_type=F32
        ).astype(BF16)
    cur[...] = in_planes(0, TX).reshape(NT, TX, COLS)

    for k in range(2):
        wide = vol_ref[0, HALO * k : HALO * k + HALO].astype(F32)[12 * k : 12 * k + EDGE]
        edge_out[k] = jnp.concatenate(
            [wide[:, QUARTER * q : QUARTER * q + QUARTER] for q in range(4)], axis=0
        ).astype(BF16)
    pl.semaphore_wait(
        barrier,
        NT - 1
        + 3 * (has_lo.astype(I32) + has_hi.astype(I32))
        + (NT - 1) * (below.astype(I32) + above.astype(I32)),
    )

    def halo(ds):
        k = 0 if ds < 0 else 1
        return remote(
            edge_out.at[k], edge.at[1 - k], halo_send.at[k], halo_recv.at[k], (t, s + ds)
        )

    def raw_copy(k):
        to = peer(k)
        return remote(
            vol_ref.at[0, :, columns(to)], raw.at[t, pl.ds(HALO, TX)],
            raw_send.at[k], raw_recv.at[k], (to, s),
        )

    def cur_copy(k):
        to = lax.rem(x + k, 4)
        return remote(
            cur.at[pl.ds(4 * to, 4)], got.at[x], cur_send.at[k], cur_recv.at[k],
            (4 * to + z, s),
        )

    for ds in (-1, 1):
        pl.when(there[ds])(halo(ds).start)
    def move_copy(ds):
        return remote(move, moved, move_send, move_recv, (t, s + ds))

    for ds in (-1, 1):
        pl.when(far[ds])(move_copy(ds).start)
    for k in (2, 1, 3):
        cur_copy(k).start()
    each_peer(lambda k: raw_copy(k).start())

    def far_copy(k, ds):
        to = t if k == NT - 1 else peer(k)
        src, dst = (0, 48) if ds < 0 else (HALO, 0)
        return remote(
            vol_ref.at[0, pl.ds(src, HALO), columns(to)], raw.at[t, pl.ds(dst, HALO)],
            far_send.at[k], far_recv.at[k], (to, s + ds),
        )

    def each_far(act, where):
        for ds in (-1, 1):

            @pl.when(where[ds])
            def _():
                for k in range(NT):
                    getattr(far_copy(k, ds), act)()

    each_far("start", far)
    got[x] = cur[pl.ds(4 * x, 4)]
    raw[t, HALO : HALO + TX] = vol_ref[0, :, columns(t)]

    for k, ds, at in ((0, -1, 0), (1, 1, 48)):

        @pl.when(jnp.logical_not(there[ds]))
        def _():
            edge[k] = jnp.zeros((HALO, QUARTER), BF16)
            raw[:, at : at + HALO] = jnp.zeros((NT, HALO, COLS), BF16)
            win[:, :, at : at + HALO] = jnp.zeros((2, 3, HALO, COLS), BF16)

    row = lax.broadcasted_iota(I32, (TX, PL), 0)
    col = lax.broadcasted_iota(I32, (TX, PL), 1)
    for part_of in range(4):
        across[part_of] = band(
            shift_ref[1, 0, 0, 0], row - source_of(col, part_of)
        ).astype(BF16)
    row = lax.broadcasted_iota(I32, (HALO, TX), 0)
    row = jnp.where(row < EDGE, row, jnp.where(row < 8, row + 24, 8 * PL))
    col = lax.broadcasted_iota(I32, (HALO, TX), 1) + TX
    from_margins = [
        band(shift_ref[0, 0, 0, 0], row - source_of(col, part_of)).astype(BF16)
        for part_of in range(4)
    ]
    plane_tables(1)
    for k in (1, 3, 2):
        cur_copy(k).wait_recv()
    sums[...] = jnp.sum(got[...].astype(F32), axis=0).astype(BF16)

    def share_copy(k):
        to = 4 * x + lax.rem(z + k, 4)
        return remote(
            sums.at[snake(to) - 4 * x], shares.at[z], share_send.at[k], share_recv.at[k], (to, s)
        )

    for k in (2, 1, 3):
        share_copy(k).start()
    shares[z] = sums[chunk - 4 * x]

    for ds in (-1, 1):
        pl.when(from_side[ds])(halo(ds).wait_recv)

    for c in range(NT):
        at = (c % 4) * COLS
        rows = jnp.concatenate([edge[k, :, at : at + COLS] for k in range(2)], axis=0)
        xw[(c + 2) * HALO : (c + 3) * HALO] = jnp.dot(
            from_margins[c // 4], rows, preferred_element_type=F32
        ).astype(BF16)
    xw[18 * HALO : 19 * HALO] = jnp.zeros((HALO, COLS), BF16)
    eight = in_planes(0, HALO, F32).reshape(NT, HALO, COLS)[:, 0:8]
    rest[...] = jnp.concatenate([eight[:, :, :128], eight[:, :, 128:]], axis=1).astype(BF16)

    def rest_copy(k):
        to = peer(k)
        return remote(rest.at[snake(to)], rests.at[t], rest_send.at[k], rest_recv.at[k], (to, s))

    each_peer(lambda k: rest_copy(k).start())
    rests[t] = rest[chunk]

    at_far = below | above
    m = below.astype(I32)

    def over_copy(k):
        to = peer(k)
        return remote(over.at[snake(to)], overs.at[t], over_send.at[k], over_recv.at[k], (to, s))

    @pl.when(at_far)
    def _():
        for ds in (-1, 1):
            pl.when(from_far[ds])(move_copy(ds).wait_recv)
        shift = [
            jnp.concatenate([moved[k : k + 1, :]] * 2, axis=1) for k in range(3)
        ]
        third = band(shift[2], (b & 63) - (a & 63))
        for d in range(4):
            second = band(shift[1], (b >> 6) - (a >> 6) - 4 * (d - 2))
            far_planes[d] = (second * third).astype(BF16)
        row = lax.broadcasted_iota(I32, (HALO, TX), 0)
        col = lax.broadcasted_iota(I32, (HALO, TX), 1)
        after = jnp.where(row < 4, row + TX, 8 * PL)
        before = jnp.where((row >= 4) & (row < 8), row - 8, 8 * PL)
        weight = band(moved[0:1, 0:TX], m * after + (1 - m) * before - col).astype(BF16)
        for c in range(NT):
            xw[(c + 2) * HALO : (c + 3) * HALO] = jnp.dot(
                weight, vol_ref[0, :, c * COLS : (c + 1) * COLS], preferred_element_type=F32
            ).astype(BF16)
        total = jnp.dot(xw[0 : NT * HALO], far_planes[0], preferred_element_type=F32)
        for d in range(1, 4):
            total += jnp.dot(
                xw[d * HALO : (d + NT) * HALO], far_planes[d], preferred_element_type=F32
            )
        eight = total.reshape(NT, HALO, COLS)[:, 0:8]
        over[...] = jnp.concatenate([eight[:, :, :128], eight[:, :, 128:]], axis=1).astype(BF16)
        each_peer(lambda k: over_copy(k).start())
        overs[t] = over[chunk]

    @pl.when(jnp.logical_not(at_far))
    def _():
        extras[...] = jnp.zeros((3, HALO, COLS), BF16)

    def extra_copy(dt):
        k = (dt + 1) // 2
        return remote(
            extras.at[1], extras.at[1 - dt], extra_send.at[k], extra_recv.at[k], (beside(dt), s)
        )

    def win_copy(i, side, act):
        dt, ds = SIDES[side]
        src = {0: HALO, -1: HALO, 1: TX}[ds]
        dst = {0: HALO, -1: 48, 1: 0}[ds]
        rows = TX if ds == 0 else HALO
        copy = remote(
            win.at[i, 1, pl.ds(src, rows)], win.at[i, 1 - dt, pl.ds(dst, rows)],
            win_send.at[i, side], win_recv.at[i, side], (beside(dt), s + ds),
        )
        present = (from_side if act == "wait_recv" else there).get(ds)
        if present is None:
            getattr(copy, act)()
        elif i == 1 and act == "start":
            pl.when(present & jnp.logical_not(far[ds]))(copy.start)
        else:
            pl.when(present)(getattr(copy, act))

    def far_win_copy(side):
        dt, ds = SIDES[side]
        src, dst = (0, 48) if ds < 0 else (HALO, 0)
        return remote(
            apart.at[pl.ds(src, HALO)], win.at[1, 1 - dt, pl.ds(dst, HALO)],
            win_send.at[1, side], win_recv.at[1, side], (beside(dt), s + ds),
        )

    def windows(i, mean):
        win[i, 1, HALO : HALO + TX] = mean.astype(BF16)
        for side in range(8):
            win_copy(i, side, "start")

    each_peer(lambda k: raw_copy(k).wait_recv())
    windows(0, jnp.sum(raw[:, HALO : HALO + TX].astype(F32), axis=0) * (1.0 / NT))

    def rim(ds):
        src, dst = (HALO, 48) if ds < 0 else (TX, 0)
        k = 0 if ds < 0 else 1
        return remote(
            raw.at[:, pl.ds(src, HALO)], raw.at[:, pl.ds(dst, HALO)],
            rim_send.at[k], rim_recv.at[k], (t, s + ds),
        )

    near = {ds: there[ds] & jnp.logical_not(far[ds]) for ds in (-1, 1)}
    from_near = {ds: from_side[ds] & jnp.logical_not(from_far[ds]) for ds in (-1, 1)}
    for ds in (-1, 1):
        pl.when(near[ds])(rim(ds).start)

    xw[0:64] = jnp.zeros((64, COLS), BF16)
    xw[18 * TX : 19 * TX] = jnp.zeros((TX, COLS), BF16)
    for c in range(NT):
        at = (c % 4) * COLS
        rows = [vol_ref[0, :, c * COLS : (c + 1) * COLS]]
        rows += [edge[k, :, at : at + COLS] for k in range(2)]
        xw[(c + 2) * TX : (c + 3) * TX] = jnp.dot(
            across[c // 4], jnp.concatenate(rows, axis=0), preferred_element_type=F32
        ).astype(BF16)
    second_warp = in_planes(1, TX)
    for c in range(NT):
        reg_ref[0, :, c * COLS : (c + 1) * COLS] = second_warp[c * TX : (c + 1) * TX]

    for k in (1, 3, 2):
        share_copy(k).wait_recv()
    mean = jnp.sum(shares[...].astype(F32), axis=0)

    @pl.when(at_far)
    def _():
        apart[...] = (mean * (1.0 / NT)).astype(BF16)
        for side in range(8):
            if SIDES[side][1]:
                pl.when(far[SIDES[side][1]])(far_win_copy(side).start)

    each_peer(lambda k: rest_copy(k).wait_recv())
    added = jnp.sum(rests[...].astype(F32), axis=0)
    added = jnp.concatenate([added[0:8], added[8:16]], axis=1)
    first = lax.broadcasted_iota(I32, (8, COLS), 0) < EDGE
    mean = jnp.concatenate(
        [
            mean[0:8] + jnp.where(first, added, 0.0),
            mean[8:24],
            mean[24:32] + jnp.where(first, 0.0, added),
        ],
        axis=0,
    ) * (1.0 / NT)
    windows(1, mean)
    to_place = remote(
        mean_out, tmpl_ref, mean_send, mean_recv, (chunk, s)
    )

    mean_out[...] = mean
    put_mean = pltpu.make_async_copy(mean_out, tmpl_ref, local_sem)
    pl.when(chunk == t)(put_mean.start)
    pl.when(chunk != t)(to_place.start)

    @pl.when(at_far)
    def _():
        each_peer(lambda k: over_copy(k).wait_recv())
        x16 = jnp.sum(overs[...].astype(F32), axis=0) * (1.0 / NT)
        x8 = jnp.concatenate([x16[0:8], x16[8:16]], axis=1)
        extras[1] = jnp.concatenate([x8, jnp.zeros_like(x8)], axis=0).astype(BF16)
        for dt in (-1, 1):
            extra_copy(dt).start()

    for ds in (-1, 1):
        pl.when(from_near[ds])(rim(ds).wait_recv)
    each_far("wait_recv", from_far)
    for j in range(8):
        rows16 = raw[:, 16 * (j // 2) : 16 * (j // 2) + 16].astype(F32)
        eight = rows16[:, 8 * (j % 2) : 8 * (j % 2) + 8].reshape(NT * 8, COLS)
        turned[j] = eight.T.astype(BF16)

    lane = lax.broadcasted_iota(I32, (PL, 128), 1)
    place = lane & 63
    low_half = lane < 64
    step_of = lax.broadcasted_iota(I32, (128, 128), 1) & 7
    owner = lax.broadcasted_iota(I32, (NT, 128), 1) >> 3
    pick = (owner == lax.broadcasted_iota(I32, (NT, 128), 0)).astype(BF16)

    def correlate(i):
        windows = [win[i, k].astype(F32) for k in range(3)]
        if i == 1:
            mf = m.astype(F32)
            for k in range(3):
                x8 = extras[k].astype(F32)[0:8]
                w = windows[k]
                windows[k] = jnp.concatenate(
                    [w[0:8], w[8:16] + (1.0 - mf) * x8, w[16:48], w[48:56] + mf * x8, w[56:64]],
                    axis=0,
                )
        blocks = []
        for half in range(6):
            x = windows[half // 2][:, 128 * (half % 2) : 128 * (half % 2) + 128]
            blocks.append(pltpu.roll(x, 3, 0))

        def both(x):
            return jnp.concatenate([x, x[8:], x[:8]], axis=0).astype(BF16)

        for j3 in range(8):
            lag = j3 - 4
            turn = [pltpu.roll(x, lag % 128, 1) if lag else x for x in blocks]
            other = [pltpu.roll(x, (lag + 64) % 128, 1) for x in blocks]
            if lag > 0:
                inside = place >= lag
            else:
                inside = place < PL + lag
            even = [jnp.where(inside, p, q) for p, q in zip(turn, other)]
            swapped = [jnp.where(inside, q, p) for p, q in zip(turn, other)]
            odd = [
                both(jnp.where(low_half, swapped[h], swapped[h + 1])) for h in range(5)
            ]
            even = [x if h == 0 else both(x) for h, x in enumerate(even)]
            total = jnp.zeros((128, 128), F32)
            for j in range(8):
                rows = slice((j % 2) * PL + 16 * (j // 2), (j % 2) * PL + 16 * (j // 2) + 16)
                stack = []
                for j2 in range(8):
                    off = 8 - j2
                    which = odd if off % 2 else even
                    h = off // 2
                    stack.append(jnp.concatenate([which[h][rows], which[h + 1][rows]], axis=1))
                total += jnp.dot(
                    jnp.concatenate(stack, axis=0), turned[j], preferred_element_type=F32
                )
            for bit in (1, 2, 4):
                total = jnp.where((step_of & bit) != 0, pltpu.roll(total, 128 - bit, 0), total)
            lagged[j3 * 64 : (j3 + 1) * 64] = total.reshape(8, 16, 128)[:, 0:8].reshape(64, 128)
        ordered = jnp.concatenate(
            [
                lagged[pl.ds(j2 * 8 + 7 - j1, 8, stride=64), :]
                for j1 in range(8)
                for j2 in range(8)
            ],
            axis=0,
        )
        upper = ordered.astype(BF16)
        lower = (ordered - upper.astype(F32)).astype(BF16)
        sums = sum(
            lax.dot_general(
                pick, x, (((1,), (1,)), ((), ())), preferred_element_type=F32
            )
            for x in (upper, lower)
        ) * (1.0 / float(PL) ** 3)
        for k in range(4):
            part[:, 4 * i + k, :] = sums[:, 128 * k : 128 * k + 128]

    for i in range(2):
        for side in range(8):
            win_copy(i, side, "wait_recv")
        if i == 1:

            @pl.when(at_far)
            def _():
                for dt in (-1, 1):
                    extra_copy(dt).wait_recv()

        correlate(i)

    def part_copy(k):
        to = peer(k)
        return remote(part.at[to], gath.at[t], part_send.at[k], part_recv.at[k], (to, s))

    each_peer(lambda k: part_copy(k).start())
    gath[t] = part[t]
    for ds in (-1, 1):
        pl.when(there[ds])(halo(ds).wait_send)
        pl.when(near[ds])(rim(ds).wait_send)
    each_far("wait_send", far)

    @pl.when(at_far)
    def _():
        each_peer(lambda k: over_copy(k).wait_send())
        for dt in (-1, 1):
            extra_copy(dt).wait_send()
        for ds in (-1, 1):
            pl.when(far[ds])(move_copy(ds).wait_send)

    each_peer(lambda k: raw_copy(k).wait_send())
    for k in range(1, 4):
        cur_copy(k).wait_send()
        share_copy(k).wait_send()
    each_peer(lambda k: rest_copy(k).wait_send())
    for i in range(2):
        for side in range(8):
            win_copy(i, side, "wait_send")
    each_peer(lambda k: part_copy(k).wait_recv())
    final = jnp.sum(gath[...], axis=0)
    for i in range(2):
        for k in range(4):
            corr_ref[i, 0, :, 128 * k : 128 * k + 128] = final[4 * i + k : 4 * i + k + 1]
    each_peer(lambda k: part_copy(k).wait_send())
    pl.when(chunk == t)(put_mean.wait)
    pl.when(chunk != t)(to_place.wait)


def put(*refs):
    *arrays, sems = refs
    copies = [pltpu.make_async_copy(arrays[k], arrays[k + 3], sems.at[k]) for k in range(3)]
    for copy in copies:
        copy.start()
    for copy in copies:
        copy.wait()


def solution(mesh):
    ns = mesh.shape["space"]

    def on_device(volumes, shifts):
        dma = pltpu.SemaphoreType.DMA
        vmem = pltpu.VMEM
        results = pl.pallas_call(
            functools.partial(kernel, ns),
            out_shape=(
                jax.ShapeDtypeStruct((2, 1, 1, 512), F32),
                jax.ShapeDtypeStruct((1, TX, PL * PL), BF16),
                jax.ShapeDtypeStruct((TX, COLS), F32),
            ),
            in_specs=[
                pl.BlockSpec(memory_space=pltpu.VMEM),
                pl.BlockSpec(memory_space=pltpu.SMEM),
            ],
            out_specs=(
                pl.BlockSpec(memory_space=pltpu.VMEM),
                pl.BlockSpec(memory_space=pltpu.VMEM),
                pl.BlockSpec(memory_space=pltpu.VMEM),
            ),
            scratch_shapes=[
                vmem((2, HALO, QUARTER), BF16),
                vmem((2, HALO, QUARTER), BF16),
                vmem((NT, PL, COLS), BF16),
                vmem((4, TX, PL), BF16),
                vmem((2, 4, COLS, COLS), BF16),
                vmem(((NT + 3) * TX, COLS), BF16),
                vmem((NT, TX, COLS), BF16),
                vmem((4, 4, TX, COLS), BF16),
                vmem((4, TX, COLS), BF16),
                vmem((4, TX, COLS), BF16),
                vmem((NT, HALO, 128), BF16),
                vmem((NT, HALO, 128), BF16),
                vmem((NT, HALO, 128), BF16),
                vmem((NT, HALO, 128), BF16),
                vmem((3, HALO, COLS), BF16),
                vmem((TX, COLS), BF16),
                vmem((8, 128), I32),
                vmem((8, 128), I32),
                vmem((4, COLS, COLS), BF16),
                vmem((2, 3, PL, COLS), BF16),
                vmem((8, COLS, 128), BF16),
                vmem((TX, COLS), F32),
                vmem((512, 128), F32),
                vmem((NT, 8, 128), F32),
                vmem((NT, 8, 128), F32),
                dma,
                dma((2,)), dma((2,)),
                dma((NT,)), dma((NT,)),
                dma((2,)), dma((2,)),
                dma((4,)), dma((4,)),
                dma((4,)), dma((4,)),
                dma((NT,)), dma((NT,)),
                dma((NT,)), dma((NT,)),
                dma((NT,)), dma((NT,)),
                dma((2,)), dma((2,)),
                dma, dma,
                dma((2, 8)), dma((2, 8)),
                dma, dma,
                dma((NT,)), dma((NT,)),
            ],
            compiler_params=pltpu.CompilerParams(
                collective_id=0, has_side_effects=True, vmem_limit_bytes=40 * 1024 * 1024
            ),
        )(volumes, shifts.transpose(0, 2, 3, 1))
        return pl.pallas_call(
            put,
            out_shape=tuple(jax.ShapeDtypeStruct(x.shape, x.dtype) for x in results),
            in_specs=[pl.BlockSpec(memory_space=pl.ANY)] * 3,
            out_specs=(pl.BlockSpec(memory_space=pl.ANY),) * 3,
            scratch_shapes=[dma((3,))],
            compiler_params=pltpu.CompilerParams(vmem_limit_bytes=1024 * 1024),
        )(*results)

    return jax.shard_map(
        on_device,
        mesh=mesh,
        in_specs=(P("tm", "space", None), P(None, None, "tm", "space")),
        out_specs=(P(None, "tm", "space", None), P("tm", "space", None), P("space", "tm")),
        check_vma=False,
    )
```

```python
import functools

import jax
import jax.numpy as jnp
from jax import lax
from jax.experimental import pallas as pl
from jax.experimental.pallas import tpu as pltpu
from jax.sharding import PartitionSpec as P

MESH = pl.DeviceIdType.MESH
F32, BF16, I32 = jnp.float32, jnp.bfloat16, jnp.int32

PL = 64
TX = 32
HALO = 16
NT = 16
COLS = 256
EDGE = 4
QUARTER = PL * PL // 4
OFFSETS = (
    (2, 2), (2, 1), (2, 3), (1, 2), (3, 2), (1, 1), (1, 3), (3, 1), (3, 3),
    (0, 2), (0, 1), (0, 3), (2, 0), (1, 0), (3, 0),
)
SIDES = tuple((dt, ds) for ds in (-1, 1, 0) for dt in (-1, 0, 1) if (dt, ds) != (0, 0))


def band(shift, delta):
    whole = jnp.right_shift(shift, 2)
    fraction = (shift - 4 * whole).astype(F32) * 0.25
    return jnp.where(
        delta == whole, 1.0 - fraction, jnp.where(delta == whole + 1, fraction, 0.0)
    )


def snake(t):
    z = lax.rem(t, 4)
    return t + lax.rem(t // 4, 2) * (3 - 2 * z)


def kernel(
    ns, vol_ref, shift_ref, corr_ref, reg_ref, tmpl_ref,
    edge_out, edge, raw, across, planes, xw, cur, got, sums, shares, rest, rests, over, overs, extras, apart, move, moved, far_planes, win, turned, mean_out,
    lagged, part, gath,
    local_sem, halo_send, halo_recv, raw_send, raw_recv, rim_send, rim_recv,
    cur_send, cur_recv, share_send, share_recv, rest_send, rest_recv, far_send, far_recv, over_send, over_recv, extra_send, extra_recv, move_send, move_recv,
    win_send, win_recv, mean_send, mean_recv, part_send, part_recv,
):
    t = lax.axis_index("tm")
    s = lax.axis_index("space")
    chunk = snake(t)
    has_lo, has_hi = s > 0, s < ns - 1
    there = {-1: has_lo, 1: has_hi}
    from_side = {-1: has_hi, 1: has_lo}
    below, above = s == ns // 2 - 1, s == ns // 2
    far = {-1: above, 1: below}
    from_far = {-1: below, 1: above}

    def peer(k):
        dx, dz = OFFSETS[k]
        return 4 * lax.rem(t // 4 + dx, 4) + lax.rem(lax.rem(t, 4) + dz, 4)

    def beside(dt):
        return snake(lax.rem(chunk + dt + NT, NT))

    x, z = t // 4, lax.rem(t, 4)

    def columns(to):
        return pl.ds(pl.multiple_of(snake(to) * COLS, COLS), COLS)

    def each_peer(body):
        for k in range(NT - 1):
            body(k)

    def remote(src, dst, send, recv, peer):
        return pltpu.make_async_remote_copy(
            src_ref=src, dst_ref=dst, send_sem=send, recv_sem=recv,
            device_id=peer, device_id_type=MESH,
        )

    barrier = pltpu.get_barrier_semaphore()
    each_peer(
        lambda k: pl.semaphore_signal(
            barrier, inc=1, device_id=(peer(k), s), device_id_type=MESH
        )
    )
    for ds in (-1, 1):

        @pl.when(there[ds])
        def _():
            for dt in (-1, 0, 1):
                pl.semaphore_signal(
                    barrier, inc=1, device_id=(beside(dt), s + ds), device_id_type=MESH
                )

    for ds in (-1, 1):

        @pl.when(far[ds])
        def _():
            for k in range(NT - 1):
                pl.semaphore_signal(
                    barrier, inc=1, device_id=(peer(k), s + ds), device_id_type=MESH
                )

    def source_of(col, part):
        margin = jnp.where(col < 48, -EDGE, TX) + (col & 3)
        return jnp.where(col < TX, col, jnp.where((col & 15) >> 2 == part, margin, 2 * PL))

    a = lax.broadcasted_iota(I32, (COLS, COLS), 0)
    b = lax.broadcasted_iota(I32, (COLS, COLS), 1)

    def plane_tables(i):
        third = band(shift_ref[i, 0, 0, 2], (b & 63) - (a & 63))
        for d in range(4):
            second = band(shift_ref[i, 0, 0, 1], (b >> 6) - (a >> 6) - 4 * (d - 2))
            planes[i, d] = (second * third).astype(BF16)

    def in_planes(i, n, dtype=BF16):
        total = jnp.dot(xw[0 : NT * n], planes[i, 0], preferred_element_type=F32)
        for d in range(1, 4):
            total += jnp.dot(
                xw[d * n : (d + NT) * n], planes[i, d], preferred_element_type=F32
            )
        return total.astype(dtype)

    row = lax.broadcasted_iota(I32, (8, 128), 0)
    move[...] = jnp.where(
        row == 0, shift_ref[0, 0, 0, 0], jnp.where(row == 1, shift_ref[0, 0, 0, 1], shift_ref[0, 0, 0, 2])
    )
    plane_tables(0)
    row = lax.broadcasted_iota(I32, (TX, TX), 0)
    col = lax.broadcasted_iota(I32, (TX, TX), 1)
    from_own = band(shift_ref[0, 0, 0, 0], row - col).astype(BF16)
    xw[0:64] = jnp.zeros((64, COLS), BF16)
    xw[18 * TX : 19 * TX] = jnp.zeros((TX, COLS), BF16)
    for c in range(NT):
        xw[(c + 2) * TX : (c + 3) * TX] = jnp.dot(
            from_own, vol_ref[0, :, c * COLS : (c + 1) * COLS], preferred_element_type=F32
        ).astype(BF16)
    cur[...] = in_planes(0, TX).reshape(NT, TX, COLS)

    for k in range(2):
        wide = vol_ref[0, HALO * k : HALO * k + HALO].astype(F32)[12 * k : 12 * k + EDGE]
        edge_out[k] = jnp.concatenate(
            [wide[:, QUARTER * q : QUARTER * q + QUARTER] for q in range(4)], axis=0
        ).astype(BF16)
    pl.semaphore_wait(
        barrier,
        NT - 1
        + 3 * (has_lo.astype(I32) + has_hi.astype(I32))
        + (NT - 1) * (below.astype(I32) + above.astype(I32)),
    )

    def halo(ds):
        k = 0 if ds < 0 else 1
        return remote(
            edge_out.at[k], edge.at[1 - k], halo_send.at[k], halo_recv.at[k], (t, s + ds)
        )

    def raw_copy(k):
        to = peer(k)
        return remote(
            vol_ref.at[0, :, columns(to)], raw.at[t, pl.ds(HALO, TX)],
            raw_send.at[k], raw_recv.at[k], (to, s),
        )

    def cur_copy(k):
        to = lax.rem(x + k, 4)
        return remote(
            cur.at[pl.ds(4 * to, 4)], got.at[x], cur_send.at[k], cur_recv.at[k],
            (4 * to + z, s),
        )

    for ds in (-1, 1):
        pl.when(there[ds])(halo(ds).start)
    def move_copy(ds):
        return remote(move, moved, move_send, move_recv, (t, s + ds))

    for ds in (-1, 1):
        pl.when(far[ds])(move_copy(ds).start)
    for k in (2, 1, 3):
        cur_copy(k).start()
    each_peer(lambda k: raw_copy(k).start())

    def far_copy(k, ds):
        to = t if k == NT - 1 else peer(k)
        src, dst = (0, 48) if ds < 0 else (HALO, 0)
        return remote(
            vol_ref.at[0, pl.ds(src, HALO), columns(to)], raw.at[t, pl.ds(dst, HALO)],
            far_send.at[k], far_recv.at[k], (to, s + ds),
        )

    def each_far(act, where):
        for ds in (-1, 1):

            @pl.when(where[ds])
            def _():
                for k in range(NT):
                    getattr(far_copy(k, ds), act)()

    each_far("start", far)
    got[x] = cur[pl.ds(4 * x, 4)]
    raw[t, HALO : HALO + TX] = vol_ref[0, :, columns(t)]

    for k, ds, at in ((0, -1, 0), (1, 1, 48)):

        @pl.when(jnp.logical_not(there[ds]))
        def _():
            edge[k] = jnp.zeros((HALO, QUARTER), BF16)
            raw[:, at : at + HALO] = jnp.zeros((NT, HALO, COLS), BF16)
            win[:, :, at : at + HALO] = jnp.zeros((2, 3, HALO, COLS), BF16)

    row = lax.broadcasted_iota(I32, (TX, PL), 0)
    col = lax.broadcasted_iota(I32, (TX, PL), 1)
    for part_of in range(4):
        across[part_of] = band(
            shift_ref[1, 0, 0, 0], row - source_of(col, part_of)
        ).astype(BF16)
    row = lax.broadcasted_iota(I32, (HALO, TX), 0)
    row = jnp.where(row < EDGE, row, jnp.where(row < 8, row + 24, 8 * PL))
    col = lax.broadcasted_iota(I32, (HALO, TX), 1) + TX
    from_margins = [
        band(shift_ref[0, 0, 0, 0], row - source_of(col, part_of)).astype(BF16)
        for part_of in range(4)
    ]
    plane_tables(1)
    for k in (1, 3, 2):
        cur_copy(k).wait_recv()
    sums[...] = jnp.sum(got[...].astype(F32), axis=0).astype(BF16)

    def share_copy(k):
        to = 4 * x + lax.rem(z + k, 4)
        return remote(
            sums.at[snake(to) - 4 * x], shares.at[z], share_send.at[k], share_recv.at[k], (to, s)
        )

    for k in (2, 1, 3):
        share_copy(k).start()
    shares[z] = sums[chunk - 4 * x]

    for ds in (-1, 1):
        pl.when(from_side[ds])(halo(ds).wait_recv)

    for c in range(NT):
        at = (c % 4) * COLS
        rows = jnp.concatenate([edge[k, :, at : at + COLS] for k in range(2)], axis=0)
        xw[(c + 2) * HALO : (c + 3) * HALO] = jnp.dot(
            from_margins[c // 4], rows, preferred_element_type=F32
        ).astype(BF16)
    xw[18 * HALO : 19 * HALO] = jnp.zeros((HALO, COLS), BF16)
    eight = in_planes(0, HALO, F32).reshape(NT, HALO, COLS)[:, 0:8]
    rest[...] = jnp.concatenate([eight[:, :, :128], eight[:, :, 128:]], axis=1).astype(BF16)

    def rest_copy(k):
        to = peer(k)
        return remote(rest.at[snake(to)], rests.at[t], rest_send.at[k], rest_recv.at[k], (to, s))

    each_peer(lambda k: rest_copy(k).start())
    rests[t] = rest[chunk]

    at_far = below | above
    m = below.astype(I32)

    def over_copy(k):
        to = peer(k)
        return remote(over.at[snake(to)], overs.at[t], over_send.at[k], over_recv.at[k], (to, s))

    @pl.when(at_far)
    def _():
        for ds in (-1, 1):
            pl.when(from_far[ds])(move_copy(ds).wait_recv)
        shift = [
            jnp.concatenate([moved[k : k + 1, :]] * 2, axis=1) for k in range(3)
        ]
        third = band(shift[2], (b & 63) - (a & 63))
        for d in range(4):
            second = band(shift[1], (b >> 6) - (a >> 6) - 4 * (d - 2))
            far_planes[d] = (second * third).astype(BF16)
        row = lax.broadcasted_iota(I32, (HALO, TX), 0)
        col = lax.broadcasted_iota(I32, (HALO, TX), 1)
        after = jnp.where(row < 4, row + TX, 8 * PL)
        before = jnp.where((row >= 4) & (row < 8), row - 8, 8 * PL)
        weight = band(moved[0:1, 0:TX], m * after + (1 - m) * before - col).astype(BF16)
        for c in range(NT):
            xw[(c + 2) * HALO : (c + 3) * HALO] = jnp.dot(
                weight, vol_ref[0, :, c * COLS : (c + 1) * COLS], preferred_element_type=F32
            ).astype(BF16)
        total = jnp.dot(xw[0 : NT * HALO], far_planes[0], preferred_element_type=F32)
        for d in range(1, 4):
            total += jnp.dot(
                xw[d * HALO : (d + NT) * HALO], far_planes[d], preferred_element_type=F32
            )
        eight = total.reshape(NT, HALO, COLS)[:, 0:8]
        over[...] = jnp.concatenate([eight[:, :, :128], eight[:, :, 128:]], axis=1).astype(BF16)
        each_peer(lambda k: over_copy(k).start())
        overs[t] = over[chunk]

    @pl.when(jnp.logical_not(at_far))
    def _():
        extras[...] = jnp.zeros((3, HALO, COLS), BF16)

    def extra_copy(dt):
        k = (dt + 1) // 2
        return remote(
            extras.at[1], extras.at[1 - dt], extra_send.at[k], extra_recv.at[k], (beside(dt), s)
        )

    def win_copy(i, side, act):
        dt, ds = SIDES[side]
        src = {0: HALO, -1: HALO, 1: TX}[ds]
        dst = {0: HALO, -1: 48, 1: 0}[ds]
        rows = TX if ds == 0 else HALO
        copy = remote(
            win.at[i, 1, pl.ds(src, rows)], win.at[i, 1 - dt, pl.ds(dst, rows)],
            win_send.at[i, side], win_recv.at[i, side], (beside(dt), s + ds),
        )
        present = (from_side if act == "wait_recv" else there).get(ds)
        if present is None:
            getattr(copy, act)()
        elif i == 1 and act == "start":
            pl.when(present & jnp.logical_not(far[ds]))(copy.start)
        else:
            pl.when(present)(getattr(copy, act))

    def far_win_copy(side):
        dt, ds = SIDES[side]
        src, dst = (0, 48) if ds < 0 else (HALO, 0)
        return remote(
            apart.at[pl.ds(src, HALO)], win.at[1, 1 - dt, pl.ds(dst, HALO)],
            win_send.at[1, side], win_recv.at[1, side], (beside(dt), s + ds),
        )

    def windows(i, mean):
        win[i, 1, HALO : HALO + TX] = mean.astype(BF16)
        for side in range(8):
            win_copy(i, side, "start")

    each_peer(lambda k: raw_copy(k).wait_recv())
    windows(0, jnp.sum(raw[:, HALO : HALO + TX].astype(F32), axis=0) * (1.0 / NT))

    def rim(ds):
        src, dst = (HALO, 48) if ds < 0 else (TX, 0)
        k = 0 if ds < 0 else 1
        return remote(
            raw.at[:, pl.ds(src, HALO)], raw.at[:, pl.ds(dst, HALO)],
            rim_send.at[k], rim_recv.at[k], (t, s + ds),
        )

    near = {ds: there[ds] & jnp.logical_not(far[ds]) for ds in (-1, 1)}
    from_near = {ds: from_side[ds] & jnp.logical_not(from_far[ds]) for ds in (-1, 1)}
    for ds in (-1, 1):
        pl.when(near[ds])(rim(ds).start)

    for k in (1, 3, 2):
        share_copy(k).wait_recv()
    mean = jnp.sum(shares[...].astype(F32), axis=0)

    @pl.when(at_far)
    def _():
        apart[...] = (mean * (1.0 / NT)).astype(BF16)
        for side in range(8):
            if SIDES[side][1]:
                pl.when(far[SIDES[side][1]])(far_win_copy(side).start)

    xw[0:64] = jnp.zeros((64, COLS), BF16)
    xw[18 * TX : 19 * TX] = jnp.zeros((TX, COLS), BF16)
    for c in range(NT):
        at = (c % 4) * COLS
        rows = [vol_ref[0, :, c * COLS : (c + 1) * COLS]]
        rows += [edge[k, :, at : at + COLS] for k in range(2)]
        xw[(c + 2) * TX : (c + 3) * TX] = jnp.dot(
            across[c // 4], jnp.concatenate(rows, axis=0), preferred_element_type=F32
        ).astype(BF16)
    second_warp = in_planes(1, TX)
    for c in range(NT):
        reg_ref[0, :, c * COLS : (c + 1) * COLS] = second_warp[c * TX : (c + 1) * TX]

    each_peer(lambda k: rest_copy(k).wait_recv())
    added = jnp.sum(rests[...].astype(F32), axis=0)
    added = jnp.concatenate([added[0:8], added[8:16]], axis=1)
    first = lax.broadcasted_iota(I32, (8, COLS), 0) < EDGE
    mean = jnp.concatenate(
        [
            mean[0:8] + jnp.where(first, added, 0.0),
            mean[8:24],
            mean[24:32] + jnp.where(first, 0.0, added),
        ],
        axis=0,
    ) * (1.0 / NT)
    windows(1, mean)
    to_place = remote(
        mean_out, tmpl_ref, mean_send, mean_recv, (chunk, s)
    )

    mean_out[...] = mean
    put_mean = pltpu.make_async_copy(mean_out, tmpl_ref, local_sem)
    pl.when(chunk == t)(put_mean.start)
    pl.when(chunk != t)(to_place.start)

    @pl.when(at_far)
    def _():
        each_peer(lambda k: over_copy(k).wait_recv())
        x16 = jnp.sum(overs[...].astype(F32), axis=0) * (1.0 / NT)
        x8 = jnp.concatenate([x16[0:8], x16[8:16]], axis=1)
        extras[1] = jnp.concatenate([x8, jnp.zeros_like(x8)], axis=0).astype(BF16)
        for dt in (-1, 1):
            extra_copy(dt).start()

    for ds in (-1, 1):
        pl.when(from_near[ds])(rim(ds).wait_recv)
    each_far("wait_recv", from_far)
    for j in range(8):
        rows16 = raw[:, 16 * (j // 2) : 16 * (j // 2) + 16].astype(F32)
        eight = rows16[:, 8 * (j % 2) : 8 * (j % 2) + 8].reshape(NT * 8, COLS)
        turned[j] = eight.T.astype(BF16)

    lane = lax.broadcasted_iota(I32, (PL, 128), 1)
    place = lane & 63
    low_half = lane < 64
    step_of = lax.broadcasted_iota(I32, (128, 128), 1) & 7
    owner = lax.broadcasted_iota(I32, (NT, 128), 1) >> 3
    pick = (owner == lax.broadcasted_iota(I32, (NT, 128), 0)).astype(BF16)

    def correlate(i):
        windows = [win[i, k].astype(F32) for k in range(3)]
        if i == 1:
            mf = m.astype(F32)
            for k in range(3):
                x8 = extras[k].astype(F32)[0:8]
                w = windows[k]
                windows[k] = jnp.concatenate(
                    [w[0:8], w[8:16] + (1.0 - mf) * x8, w[16:48], w[48:56] + mf * x8, w[56:64]],
                    axis=0,
                )
        blocks = []
        for half in range(6):
            x = windows[half // 2][:, 128 * (half % 2) : 128 * (half % 2) + 128]
            blocks.append(pltpu.roll(x, 3, 0))

        def both(x):
            return jnp.concatenate([x, x[8:], x[:8]], axis=0).astype(BF16)

        for j3 in range(8):
            lag = j3 - 4
            turn = [pltpu.roll(x, lag % 128, 1) if lag else x for x in blocks]
            other = [pltpu.roll(x, (lag + 64) % 128, 1) for x in blocks]
            if lag > 0:
                inside = place >= lag
            else:
                inside = place < PL + lag
            even = [jnp.where(inside, p, q) for p, q in zip(turn, other)]
            swapped = [jnp.where(inside, q, p) for p, q in zip(turn, other)]
            odd = [
                both(jnp.where(low_half, swapped[h], swapped[h + 1])) for h in range(5)
            ]
            even = [x if h == 0 else both(x) for h, x in enumerate(even)]
            total = jnp.zeros((128, 128), F32)
            for j in range(8):
                rows = slice((j % 2) * PL + 16 * (j // 2), (j % 2) * PL + 16 * (j // 2) + 16)
                stack = []
                for j2 in range(8):
                    off = 8 - j2
                    which = odd if off % 2 else even
                    h = off // 2
                    stack.append(jnp.concatenate([which[h][rows], which[h + 1][rows]], axis=1))
                total += jnp.dot(
                    jnp.concatenate(stack, axis=0), turned[j], preferred_element_type=F32
                )
            for bit in (1, 2, 4):
                total = jnp.where((step_of & bit) != 0, pltpu.roll(total, 128 - bit, 0), total)
            lagged[j3 * 64 : (j3 + 1) * 64] = total.reshape(8, 16, 128)[:, 0:8].reshape(64, 128)
        ordered = jnp.concatenate(
            [
                lagged[pl.ds(j2 * 8 + 7 - j1, 8, stride=64), :]
                for j1 in range(8)
                for j2 in range(8)
            ],
            axis=0,
        )
        upper = ordered.astype(BF16)
        lower = (ordered - upper.astype(F32)).astype(BF16)
        sums = sum(
            lax.dot_general(
                pick, x, (((1,), (1,)), ((), ())), preferred_element_type=F32
            )
            for x in (upper, lower)
        ) * (1.0 / float(PL) ** 3)
        for k in range(4):
            part[:, 4 * i + k, :] = sums[:, 128 * k : 128 * k + 128]

    for i in range(2):
        for side in range(8):
            win_copy(i, side, "wait_recv")
        if i == 1:

            @pl.when(at_far)
            def _():
                for dt in (-1, 1):
                    extra_copy(dt).wait_recv()

        correlate(i)

    def part_copy(k):
        to = peer(k)
        return remote(part.at[to], gath.at[t], part_send.at[k], part_recv.at[k], (to, s))

    each_peer(lambda k: part_copy(k).start())
    gath[t] = part[t]
    for ds in (-1, 1):
        pl.when(there[ds])(halo(ds).wait_send)
        pl.when(near[ds])(rim(ds).wait_send)
    each_far("wait_send", far)

    @pl.when(at_far)
    def _():
        each_peer(lambda k: over_copy(k).wait_send())
        for dt in (-1, 1):
            extra_copy(dt).wait_send()
        for ds in (-1, 1):
            pl.when(far[ds])(move_copy(ds).wait_send)

    each_peer(lambda k: raw_copy(k).wait_send())
    for k in range(1, 4):
        cur_copy(k).wait_send()
        share_copy(k).wait_send()
    each_peer(lambda k: rest_copy(k).wait_send())
    for i in range(2):
        for side in range(8):
            win_copy(i, side, "wait_send")
    each_peer(lambda k: part_copy(k).wait_recv())
    final = jnp.sum(gath[...], axis=0)
    for i in range(2):
        for k in range(4):
            corr_ref[i, 0, :, 128 * k : 128 * k + 128] = final[4 * i + k : 4 * i + k + 1]
    each_peer(lambda k: part_copy(k).wait_send())
    pl.when(chunk == t)(put_mean.wait)
    pl.when(chunk != t)(to_place.wait)


def put(*refs):
    *arrays, sems = refs
    copies = [pltpu.make_async_copy(arrays[k], arrays[k + 3], sems.at[k]) for k in range(3)]
    for copy in copies:
        copy.start()
    for copy in copies:
        copy.wait()


def solution(mesh):
    ns = mesh.shape["space"]

    def on_device(volumes, shifts):
        dma = pltpu.SemaphoreType.DMA
        vmem = pltpu.VMEM
        results = pl.pallas_call(
            functools.partial(kernel, ns),
            out_shape=(
                jax.ShapeDtypeStruct((2, 1, 1, 512), F32),
                jax.ShapeDtypeStruct((1, TX, PL * PL), BF16),
                jax.ShapeDtypeStruct((TX, COLS), F32),
            ),
            in_specs=[
                pl.BlockSpec(memory_space=pltpu.VMEM),
                pl.BlockSpec(memory_space=pltpu.SMEM),
            ],
            out_specs=(
                pl.BlockSpec(memory_space=pltpu.VMEM),
                pl.BlockSpec(memory_space=pltpu.VMEM),
                pl.BlockSpec(memory_space=pltpu.VMEM),
            ),
            scratch_shapes=[
                vmem((2, HALO, QUARTER), BF16),
                vmem((2, HALO, QUARTER), BF16),
                vmem((NT, PL, COLS), BF16),
                vmem((4, TX, PL), BF16),
                vmem((2, 4, COLS, COLS), BF16),
                vmem(((NT + 3) * TX, COLS), BF16),
                vmem((NT, TX, COLS), BF16),
                vmem((4, 4, TX, COLS), BF16),
                vmem((4, TX, COLS), BF16),
                vmem((4, TX, COLS), BF16),
                vmem((NT, HALO, 128), BF16),
                vmem((NT, HALO, 128), BF16),
                vmem((NT, HALO, 128), BF16),
                vmem((NT, HALO, 128), BF16),
                vmem((3, HALO, COLS), BF16),
                vmem((TX, COLS), BF16),
                vmem((8, 128), I32),
                vmem((8, 128), I32),
                vmem((4, COLS, COLS), BF16),
                vmem((2, 3, PL, COLS), BF16),
                vmem((8, COLS, 128), BF16),
                vmem((TX, COLS), F32),
                vmem((512, 128), F32),
                vmem((NT, 8, 128), F32),
                vmem((NT, 8, 128), F32),
                dma,
                dma((2,)), dma((2,)),
                dma((NT,)), dma((NT,)),
                dma((2,)), dma((2,)),
                dma((4,)), dma((4,)),
                dma((4,)), dma((4,)),
                dma((NT,)), dma((NT,)),
                dma((NT,)), dma((NT,)),
                dma((NT,)), dma((NT,)),
                dma((2,)), dma((2,)),
                dma, dma,
                dma((2, 8)), dma((2, 8)),
                dma, dma,
                dma((NT,)), dma((NT,)),
            ],
            compiler_params=pltpu.CompilerParams(
                collective_id=0, has_side_effects=True, vmem_limit_bytes=40 * 1024 * 1024
            ),
        )(volumes, shifts.transpose(0, 2, 3, 1))
        return pl.pallas_call(
            put,
            out_shape=tuple(jax.ShapeDtypeStruct(x.shape, x.dtype) for x in results),
            in_specs=[pl.BlockSpec(memory_space=pl.ANY)] * 3,
            out_specs=(pl.BlockSpec(memory_space=pl.ANY),) * 3,
            scratch_shapes=[dma((3,))],
            compiler_params=pltpu.CompilerParams(vmem_limit_bytes=1024 * 1024),
        )(*results)

    return jax.shard_map(
        on_device,
        mesh=mesh,
        in_specs=(P("tm", "space", None), P(None, None, "tm", "space")),
        out_specs=(P(None, "tm", "space", None), P("tm", "space", None), P("space", "tm")),
        check_vma=False,
    )
```
